256 devices in a mesh: dp: 2 (over y_hi), expert: 128 (over y_lo, z, x, core).
Axes of the slice: x: 4, y: 4 (y_hi: 2, y_lo: 2; y = y_hi * 2 + y_lo), z: 8, core: 2. Of those that a mesh axis runs over, the one named last changes fastest.
Arguments:
- patches: bfloat16 [65536, 768], P(('dp', 'expert')), may hold values from -8 to 8
- slot_keys: bfloat16 [512, 768], P('expert'), may hold values from -2 to 2
- expert_in: bfloat16 [128, 768, 2560], P('expert', None, 'dp'), may hold values from -0.21875 to 0.21875
- expert_out: bfloat16 [128, 2560, 768], P('expert', 'dp'), may hold values from -0.125 to 0.125
- out_grad: bfloat16 [65536, 768], P(('dp', 'expert')), may hold values from -6 to 6
Outputs:
- layer_out: bfloat16 [65536, 768], P(('dp', 'expert'))
- patch_grad: bfloat16 [65536, 768], P(('dp', 'expert'))
- slot_key_grad: float32 [512, 768], P('expert')
- expert_in_grad: bfloat16 [128, 768, 2560], P('expert', None, 'dp')
- expert_out_grad: bfloat16 [128, 2560, 768], P('expert', 'dp')
The draws below stay inside these ranges and needn't reach their ends.
All inputs are finite; a program needn't handle non-finite values.
Results may differ from the reference program's by a relative error of at most 0.02.
Values may be sent and summed in bfloat16 or wider, within the bound.
No kernel may reach another device: no remote copies, remote signals or barrier semaphores. Data moves between devices by JAX's collectives and lax.ppermute only.
A program may use at most 128 MiB of HBM per device.

```python
import math
import jax
import jax.numpy as jnp
from jax import lax

D = 768
FF = 2560
SLOTS = 4
PATCH = 256
EXPERTS = 128
SLOTS_ALL = 512
IMAGES = 256
TOKENS = 65536


def draw_patches(key, part):
    own_key = jax.random.fold_in(key, 1)
    scale_key, value_key = jax.random.split(own_key)
    row_scale = jnp.exp(jax.random.uniform(scale_key, (TOKENS, 1), jnp.float32, math.log(0.25), math.log(2.5)))
    values = jax.random.truncated_normal(value_key, -3.0, 3.0, (TOKENS, D), jnp.float32) * row_scale
    return values.astype(jnp.bfloat16)


def draw_slot_keys(key, part):
    own_key = jax.random.fold_in(key, 2)
    scale_key, value_key = jax.random.split(own_key)
    slot_scale = jnp.exp(jax.random.uniform(scale_key, (SLOTS_ALL, 1), jnp.float32, math.log(0.15), math.log(1.5)))
    values = jax.random.truncated_normal(value_key, -3.0, 3.0, (SLOTS_ALL, D), jnp.float32) * slot_scale / math.sqrt(D)
    return values.astype(jnp.bfloat16)


def shard_levels(key, shape, cuts, low, high):
    def one(axis_at, shards_of):
        steps = jax.random.uniform(jax.random.fold_in(jax.random.fold_in(key, 6), axis_at), (shards_of,), jnp.float32, low / len(cuts), high / len(cuts))
        return jnp.repeat(jnp.exp(steps), shape[axis_at] // shards_of).reshape((-1,) + (1,) * (len(shape) - axis_at - 1))

    gain = one(*cuts[0])
    for cut in cuts[1:]:
        gain = gain * one(*cut)
    return gain


def scatter_about(key, dims, spread, limit, cuts=(), dtype=jnp.bfloat16):
    entries = jax.random.normal(key, dims, jnp.float32) * spread
    if len(cuts) > 0:
        entries = shard_levels(key, dims, cuts, -0.22, 0.18) * entries
    return jnp.clip(entries, min=-limit, max=limit).astype(dtype)


def setup_inputs(seed: int = 0) -> dict:
    arg_keys = jax.random.split(jax.random.key(seed), 6)
    patches = draw_patches(jax.random.fold_in(arg_keys[5], 71), 0)
    slot_keys = draw_slot_keys(jax.random.fold_in(arg_keys[5], 71), 0)
    expert_in = scatter_about(arg_keys[2], (EXPERTS, D, FF), D ** -0.5, 0.21875, ((0, 128), (2, 2)))
    expert_out = scatter_about(arg_keys[3], (EXPERTS, FF, D), FF ** -0.5, 0.125, ((0, 128), (1, 2)))
    out_grad = scatter_about(arg_keys[4], (TOKENS, D), 1.0, 6.0, ((0, 256),))
    return {"patches": patches, "slot_keys": slot_keys, "expert_in": expert_in, "expert_out": expert_out, "out_grad": out_grad}


def activation_back(projected, hidden_grad):
    return jax.vjp(jax.nn.gelu, projected)[1](hidden_grad)[0]

def softmax_along(scores, axis):
    shifted = scores - lax.optimization_barrier(jnp.max(scores, axis=axis, keepdims=True))
    raised = jnp.exp(shifted)
    return raised / lax.optimization_barrier(jnp.sum(raised, axis=axis, keepdims=True))

def softmax_back(share, share_grad, axis):
    return share * (share_grad - lax.optimization_barrier(jnp.sum(share_grad * share, axis=axis, keepdims=True)))

def to_experts(by_image):
    return by_image.reshape(IMAGES, EXPERTS, SLOTS, D).transpose(1, 0, 2, 3).reshape(EXPERTS, IMAGES * SLOTS, D)

def to_images(by_expert):
    return by_expert.reshape(EXPERTS, IMAGES, SLOTS, D).transpose(1, 0, 2, 3).reshape(IMAGES, SLOTS_ALL, D)

def reference(patches, slot_keys, expert_in, expert_out, out_grad):
    image_patches = patches.reshape(IMAGES, PATCH, D)
    image_grads = out_grad.reshape(IMAGES, PATCH, D)

    def front(image):
        scores = jnp.dot(image, slot_keys.T, preferred_element_type=jnp.float32)
        dispatch_share = softmax_along(scores, 0)
        combine_share = softmax_along(scores, 1)
        dispatch_weights = dispatch_share.astype(jnp.bfloat16)
        slot_input = jnp.dot(dispatch_weights.T, image, preferred_element_type=jnp.float32).astype(jnp.bfloat16)
        return (dispatch_share, combine_share, slot_input)
    dispatch_share, combine_share, slot_input = lax.map(front, image_patches)
    expert_rows = to_experts(slot_input)

    def forward_expert(operands):
        rows_here, first_weight, second_weight = operands
        projected = jnp.dot(rows_here, first_weight, preferred_element_type=jnp.float32)
        hidden = jax.nn.gelu(projected).astype(jnp.bfloat16)
        return jnp.dot(hidden, second_weight, preferred_element_type=jnp.float32).astype(jnp.bfloat16)
    slot_output = to_images(lax.map(forward_expert, (expert_rows, expert_in, expert_out)))

    def middle(operands):
        combine_one, slot_one, grad_one = operands
        combine_weights = combine_one.astype(jnp.bfloat16)
        layer_one = jnp.dot(combine_weights, slot_one, preferred_element_type=jnp.float32).astype(jnp.bfloat16)
        slot_out_grad = jnp.dot(combine_weights.T, grad_one, preferred_element_type=jnp.float32).astype(jnp.bfloat16)
        combine_grad = jnp.dot(grad_one, slot_one.T, preferred_element_type=jnp.float32)
        return (layer_one, slot_out_grad, softmax_back(combine_one, combine_grad, 1))
    layer_out, slot_out_grad, score_grad_mix = lax.map(middle, (combine_share, slot_output, image_grads))
    row_grads = to_experts(slot_out_grad)

    def backward_expert(operands):
        rows_here, grads_here, first_weight, second_weight = operands
        projected = jnp.dot(rows_here, first_weight, preferred_element_type=jnp.float32)
        hidden = jax.nn.gelu(projected).astype(jnp.bfloat16)
        hidden_grad = jnp.dot(grads_here, second_weight.T, preferred_element_type=jnp.float32)
        projected_grad = activation_back(projected, hidden_grad).astype(jnp.bfloat16)
        second_grad = jnp.dot(hidden.T, grads_here, preferred_element_type=jnp.float32).astype(jnp.bfloat16)
        first_grad = jnp.dot(rows_here.T, projected_grad, preferred_element_type=jnp.float32).astype(jnp.bfloat16)
        input_grads = jnp.dot(projected_grad, first_weight.T, preferred_element_type=jnp.float32).astype(jnp.bfloat16)
        return (first_grad, second_grad, input_grads)
    expert_in_grad, expert_out_grad, input_rows = lax.map(backward_expert, (expert_rows, row_grads, expert_in, expert_out))
    slot_in_grad = to_images(input_rows)

    def back(operands):
        image, dispatch_one, mix_one, input_one = operands
        dispatch_grad = jnp.dot(image, input_one.T, preferred_element_type=jnp.float32)
        score_grad = (mix_one + softmax_back(dispatch_one, dispatch_grad, 0)).astype(jnp.bfloat16)
        direct = jnp.dot(dispatch_one.astype(jnp.bfloat16), input_one, preferred_element_type=jnp.float32)
        through_keys = jnp.dot(score_grad, slot_keys, preferred_element_type=jnp.float32)
        return ((direct + through_keys).astype(jnp.bfloat16), score_grad)
    patch_grad, score_grad = lax.map(back, (image_patches, dispatch_share, score_grad_mix, slot_in_grad))
    slot_key_grad = jnp.dot(score_grad.reshape(TOKENS, SLOTS_ALL).T, patches, preferred_element_type=jnp.float32)
    return (layer_out.reshape(TOKENS, D), patch_grad.reshape(TOKENS, D), slot_key_grad, expert_in_grad, expert_out_grad)
```

```python
import jax
import jax.numpy as jnp
from jax import lax
from jax.sharding import Mesh, PartitionSpec as P

D = 768
SLOTS = 4
BF = jnp.bfloat16
F32 = jnp.float32
EXPERT = ("yl", "z", "x", "core")
TOKEN = ("dp",) + EXPERT
ROUTE = ("core", "yl", "z", "x")
PLANE = ("z", "x")


def mm(left, right, contract):
    return lax.dot_general(left, right, (contract, ((), ())), preferred_element_type=F32)


def dot(left, right):
    return mm(left, right, ((1,), (0,)))


def dot_rows(left, right):
    return mm(left, right, ((0,), (0,)))


def dot_last(left, right):
    return mm(left, right, ((1,), (1,)))


def swap(value, axis):
    return lax.ppermute(value, axis, [(0, 1), (1, 0)])


def both(value, axis):
    other = swap(value, axis)
    return jnp.where(
        lax.axis_index(axis) == 0,
        jnp.concatenate([value, other], 0),
        jnp.concatenate([other, value], 0),
    )


def halve(value, axis):
    half = value.shape[0] // 2
    low, high = value[:half], value[half:]
    first = lax.axis_index(axis) == 0
    kept = jnp.where(first, low, high)
    sent = jnp.where(first, high, low).astype(BF)
    return kept + swap(sent, axis).astype(F32)


def exchange(value, axes):
    return lax.all_to_all(value, axes, split_axis=0, concat_axis=0, tiled=True)


def gather_keys(keys):
    spread = jnp.broadcast_to(keys.reshape(1, 24, 128), (32, 24, 128))
    plane = exchange(spread, PLANE).reshape(32 * SLOTS, D)
    return both(both(plane, "yl"), "core")


def scatter_keys(term):
    plane = halve(halve(term, "core"), "yl")
    pieces = exchange(plane.astype(BF).reshape(32, SLOTS, D), PLANE)
    own = jnp.sum(pieces.astype(F32), axis=0)
    return own + swap(own, "dp")


def route(rows):
    return exchange(rows.reshape(128, SLOTS, D), ROUTE).reshape(512, D)


def softmax_parts(scores, axis):
    raised = jnp.exp(scores - jnp.max(scores, axis=axis, keepdims=True))
    return raised / jnp.sum(raised, axis=axis, keepdims=True)


def softmax_back(share, share_grad, axis):
    return share * (share_grad - jnp.sum(share_grad * share, axis=axis, keepdims=True))


def activation_back(projected, hidden_grad):
    return jax.vjp(jax.nn.gelu, projected)[1](hidden_grad)[0]


def local(patches, slot_keys, expert_in, expert_out, out_grad):
    first_weight, second_weight = expert_in[0], expert_out[0]
    keys = gather_keys(slot_keys)
    scores = dot_last(patches, keys)
    dispatch_share = softmax_parts(scores, 0)
    combine_share = softmax_parts(scores, 1)
    dispatch_weights = dispatch_share.astype(BF)
    combine_weights = combine_share.astype(BF)
    rows = route(dot_rows(dispatch_weights, patches).astype(BF))
    pair_rows = swap(rows, "dp")
    grads = route(dot_rows(combine_weights, out_grad).astype(BF))
    pair_grads = swap(grads, "dp")

    pair_projected = dot(pair_rows, first_weight)
    pair_hidden = jax.nn.gelu(pair_projected).astype(BF)
    pair_out = swap(dot(pair_hidden, second_weight).astype(BF), "dp")
    projected = dot(rows, first_weight)
    hidden = jax.nn.gelu(projected).astype(BF)
    out_rows = (dot(hidden, second_weight) + pair_out.astype(F32)).astype(BF)
    slot_output = route(out_rows)

    pair_projected_grad = activation_back(
        pair_projected, dot_last(pair_grads, second_weight)
    ).astype(BF)
    pair_in = swap(dot_last(pair_projected_grad, first_weight).astype(BF), "dp")
    projected_grad = activation_back(projected, dot_last(grads, second_weight)).astype(BF)
    in_rows = (dot_last(projected_grad, first_weight) + pair_in.astype(F32)).astype(BF)
    slot_in_grad = route(in_rows)

    second_grad = (dot_rows(hidden, grads) + dot_rows(pair_hidden, pair_grads)).astype(BF)
    first_grad = (
        dot_rows(rows, projected_grad) + dot_rows(pair_rows, pair_projected_grad)
    ).astype(BF)

    layer_out = dot(combine_weights, slot_output).astype(BF)
    combine_grad = dot_last(out_grad, slot_output)
    score_grad_mix = softmax_back(combine_share, combine_grad, 1)

    dispatch_grad = dot_last(patches, slot_in_grad)
    score_grad = (score_grad_mix + softmax_back(dispatch_share, dispatch_grad, 0)).astype(BF)
    slot_key_grad = scatter_keys(dot_rows(score_grad, patches))
    patch_grad = (dot(dispatch_weights, slot_in_grad) + dot(score_grad, keys)).astype(BF)
    return layer_out, patch_grad, slot_key_grad, first_grad[None], second_grad[None]


def solution(mesh):
    fine = Mesh(mesh.devices.reshape(2, 2, 8, 4, 2), TOKEN)
    return jax.shard_map(
        local,
        mesh=fine,
        in_specs=(
            P(TOKEN, None),
            P(EXPERT, None),
            P(EXPERT, None, "dp"),
            P(EXPERT, "dp", None),
            P(TOKEN, None),
        ),
        out_specs=(
            P(TOKEN, None),
            P(TOKEN, None),
            P(EXPERT, None),
            P(EXPERT, None, "dp"),
            P(EXPERT, "dp", None),
        ),
        check_vma=False,
    )
```

```python
import jax
import jax.numpy as jnp
from jax import lax
from jax.experimental import pallas as pl
from jax.experimental.pallas import tpu as pltpu
from jax.sharding import Mesh, PartitionSpec as P

D = 768
SLOTS = 4
BF = jnp.bfloat16
F32 = jnp.float32
EXPERT = ("yl", "z", "x", "core")
TOKEN = ("dp",) + EXPERT
ROUTE = ("core", "z", "x")
PLANE = ("z", "x", "yl")
TILE = 256
LIMIT = 46 * 1024 * 1024
SPARE = 8000000
MICRO = 1000000000
CUBIC = 0.044715
ROOT = 0.7978845608028654


def mm(left, right, contract):
    return lax.dot_general(left, right, (contract, ((), ())), preferred_element_type=F32)


def dot(left, right):
    return mm(left, right, ((1,), (0,)))


def dot_rows(left, right):
    return mm(left, right, ((0,), (0,)))


def dot_last(left, right):
    return mm(left, right, ((1,), (1,)))


class Far:
    def __init__(self, there, here, sems, first_sem, cuts):
        self.there, self.here, self.sems, self.first_sem = there, here, sems, first_sem
        self.cuts = cuts

    def copy(self, piece, out):
        rows, cols = self.here.shape
        start, stop = self.cuts[piece] if self.cuts else (0, cols)
        far = self.there.at[pl.ds(0, rows), pl.ds(start, stop - start)]
        near = self.here.at[:, pl.ds(start, stop - start)]
        source, target = (near, far) if out else (far, near)
        return pltpu.make_async_copy(source, target, self.sems.at[self.first_sem + piece])

    def fetch(self, *pieces):
        for piece in pieces or (0,):
            self.copy(piece, False).start()

    def get(self, piece=0):
        self.copy(piece, False).wait()
        start, stop = self.cuts[piece] if self.cuts else (0, self.here.shape[1])
        return self.here[:, start:stop]

    def put(self, value, piece=0):
        start, stop = self.cuts[piece] if self.cuts else (0, self.here.shape[1])
        self.here[:, start:stop] = value
        self.copy(piece, True).start()

    def wait(self):
        for piece in range(len(self.cuts or (0,))):
            self.copy(piece, True).wait()


HERE = pl.BlockSpec(memory_space=pltpu.VMEM)
FLAG = pl.BlockSpec(memory_space=pltpu.SMEM)
THERE = pl.BlockSpec(memory_space=pl.ANY)


class In:
    def __init__(self, value, rows=None, cuts=None):
        self.value, self.cuts = value, cuts
        self.shape = (rows or value.shape[0], value.shape[1])


class After:
    def __init__(self, value):
        self.value = value


class Out:
    def __init__(self, shape, dtype, cuts=None, room=False):
        self.shape, self.dtype, self.cuts = shape, dtype, cuts
        width = shape[1] * jnp.dtype(dtype).itemsize
        self.rows = max(shape[0], -(-SPARE // width) // 256 * 256 + 256) if room else shape[0]


def call(kernel, name, cost, outs, *operands):
    values, specs, scratch, plan, sems = [], [], [], [], 0

    def far(shape, dtype, cuts):
        nonlocal sems
        scratch.append(pltpu.VMEM(shape, dtype))
        sems += len(cuts or (0,))
        return len(scratch) - 1, sems - len(cuts or (0,)), cuts

    for operand in operands:
        if isinstance(operand, In):
            values.append(operand.value)
            specs.append(THERE)
            plan.append(far(operand.shape, operand.value.dtype, operand.cuts))
        elif isinstance(operand, After):
            values.append(operand.value)
            specs.append(THERE)
            plan.append(None)
        else:
            value, spec = operand if isinstance(operand, tuple) else (operand, HERE)
            values.append(value)
            specs.append(spec)
            plan.append(())
    shapes, out_specs = [], []
    for out in outs:
        if isinstance(out, Out):
            shapes.append(jax.ShapeDtypeStruct((out.rows, out.shape[1]), out.dtype))
            out_specs.append(THERE)
            plan.append(far(out.shape, out.dtype, out.cuts))
        else:
            shapes.append(jax.ShapeDtypeStruct(*out))
            out_specs.append(HERE)
            plan.append(())

    def run(*refs):
        inner, waiting = [], []
        mine = refs[len(values) + len(outs) :]
        for at, (ref, how) in enumerate(zip(refs, plan)):
            if how is None:
                continue
            if how == ():
                inner.append(ref)
                continue
            inner.append(Far(ref, mine[how[0]], mine[-1], how[1], how[2]))
            if at >= len(values):
                waiting.append(inner[-1])
        kernel(*inner)
        for one in waiting:
            one.wait()

    return pl.pallas_call(
        run,
        name=name,
        out_shape=shapes,
        in_specs=specs,
        out_specs=out_specs,
        scratch_shapes=scratch + ([pltpu.SemaphoreType.DMA((sems,))] if sems else []),
        compiler_params=pltpu.CompilerParams(vmem_limit_bytes=LIMIT),
        cost_estimate=pl.CostEstimate(flops=cost * MICRO, bytes_accessed=1000, transcendentals=0),
    )(*values)


def flat(ref):
    value = ref[...].astype(F32)
    return value.reshape(value.shape[0] * value.shape[1], D).astype(BF)


def split(value, yl):
    low, high = value[:, :SLOTS, :], value[:, SLOTS:, :]
    rows = value.shape[0] * SLOTS
    ours = jnp.where(yl == 0, low, high).reshape(rows, D)
    theirs = jnp.where(yl == 0, high, low).reshape(rows, D)
    return ours, theirs


def merge(ours, theirs, yl):
    groups = (ours.shape[0] // SLOTS, SLOTS, D)
    ours, theirs = ours.reshape(groups), theirs.reshape(groups)
    low, high = jnp.where(yl == 0, ours, theirs), jnp.where(yl == 0, theirs, ours)
    return jnp.concatenate([low, high], axis=1)


def softmax(scores, axis):
    raised = jnp.exp(scores - jnp.max(scores, axis=axis, keepdims=True))
    return raised / jnp.sum(raised, axis=axis, keepdims=True)


def softmax_back(share, share_grad, axis):
    return share * (share_grad - jnp.sum(share_grad * share, axis=axis, keepdims=True))


def front(place, patches, own, other, rows, dispatch, keys):
    patches.fetch()
    core = place[0]
    for at, block in ((core, own), (1 - core, other)):
        keys.here[pl.ds(pl.multiple_of(at * 256, 256), 256), :] = flat(block)
    keys.copy(0, True).start()
    image = patches.get()
    share = softmax(dot_last(image, keys.here[...]), 0)
    dispatch.put(share)
    rows.put(dot_rows(share.astype(BF), image).astype(BF))


def front_grads(patches, keys, out_grad, grads, combine):
    patches.fetch()
    keys.fetch()
    out_grad.fetch()
    share = softmax(dot_last(patches.get(), keys.get()), 1)
    combine.put(share)
    grads.put(dot_rows(share.astype(BF), out_grad.get()).astype(BF))


def part_ways(place, routed, ours, theirs):
    near, far = split(routed[...].astype(F32), place[1])
    ours[...] = near.astype(BF)
    theirs[...] = far.astype(BF)


def load(first, second, first_here, second_here, sems):
    copies = [
        pltpu.make_async_copy(first, first_here, sems.at[0]),
        pltpu.make_async_copy(second, second_here, sems.at[1]),
    ]
    for copy in copies:
        copy.start()
    for copy in copies:
        copy.wait()


def forward(*refs):
    blocks = (len(refs) - 3) // 2
    low, first, second, outs, acts = refs[:blocks], *refs[blocks : blocks + 2], refs[-blocks - 1 : -1], refs[-1]
    here = jnp.concatenate([ref[...] for ref in low], axis=0)
    acts.put(here, 0)
    total = None
    for start in range(0, first.shape[1], TILE):
        part = slice(start, start + TILE)
        value = dot(here, first[:, part])
        square = value * value
        bend = jnp.tanh(ROOT * value * (1.0 + CUBIC * square))
        gate = 0.5 + 0.5 * bend
        active = (value * gate).astype(BF)
        acts.put(active, 1 + start // TILE * 2)
        rise = (0.5 * ROOT) * value * (1.0 - bend * bend) * (1.0 + (3.0 * CUBIC) * square)
        acts.put((gate + rise).astype(BF), 2 + start // TILE * 2)
        term = dot(active, second[part, :])
        total = term if total is None else total + term
    for at, out in enumerate(outs):
        out[...] = total[at * 256 : at * 256 + 256].astype(out.dtype)


def backward(*refs):
    blocks = (len(refs) - 4) // 2
    low, first, second, slope, outs, kept = (
        refs[:blocks], *refs[blocks : blocks + 3], refs[-blocks - 1 : -1], refs[-1],
    )
    steps = first.shape[1] // TILE
    wanted = [2 + 2 * step for step in range(steps)]
    slope.fetch(*wanted)
    here = jnp.concatenate([ref[...] for ref in low], axis=0)
    kept.put(here, 0)
    slopes = [slope.get(piece) for piece in wanted]
    total = None
    for step in range(steps):
        part = slice(step * TILE, step * TILE + TILE)
        rounded = (dot_last(here, second[part, :]) * slopes[step].astype(F32)).astype(BF)
        kept.put(rounded, 1 + step)
        term = dot_last(rounded, first[:, part])
        total = term if total is None else total + term
    for at, out in enumerate(outs):
        out[...] = total[at * 256 : at * 256 + 256].astype(out.dtype)


def weight_grad(steps, into, *refs):
    acts, kept, out = refs[:3], refs[3:6], refs[6]
    narrow = [1 + 2 * step for step in range(steps)] if not into else [0]
    other = [0] if not into else [1 + step for step in range(steps)]
    for step in range(steps):
        for act, keep in zip(acts, kept):
            if step == 0 or not into:
                act.fetch(narrow[0 if into else step])
            if step == 0 or into:
                keep.fetch(other[step if into else 0])
    held = [(keep if not into else act).get(0) for act, keep in zip(acts, kept)]
    for step in range(steps):
        part = slice(step * TILE, step * TILE + TILE)
        total = None
        for act, keep, one in zip(acts, kept, held):
            moving = keep.get(other[step]) if into else act.get(narrow[step])
            term = dot_rows(one, moving) if into else dot_rows(moving, one)
            total = term if total is None else total + term
        if into:
            out[:, part] = total.astype(BF)
        else:
            out[part, :] = total.astype(BF)


def join(place, ours, ours_far, theirs, theirs_far, out):
    near = ours[...] + ours_far[...].astype(F32)
    far = theirs[...].astype(F32) + theirs_far[...].astype(F32)
    out[...] = merge(near, far, place[1]).astype(BF)


def middle(slot_output, out_grad, combine, layer_out, mix):
    out_grad.fetch()
    combine.fetch()
    grad = dot_last(out_grad.get(), slot_output[...])
    share = combine.get()
    mix.put(softmax_back(share, grad, 1))
    layer_out.put(dot(share.astype(BF), slot_output[...]).astype(BF))


def last(place, slot_in_grad, patches, dispatch, mix, score_grad, kept, sent, term):
    patches.fetch()
    dispatch.fetch()
    mix.fetch()
    image = patches.get()
    grad = dot_last(image, slot_in_grad[...])
    change = softmax_back(dispatch.get(), grad, 0)
    score = (mix.get() + change).astype(BF)
    score_grad.put(score)
    term[...] = dot_rows(score, image)
    core = place[0]
    kept[...] = term[pl.ds(pl.multiple_of(core * 256, 256), 256), :]
    sent[...] = term[pl.ds(pl.multiple_of((1 - core) * 256, 256), 256), :].astype(BF)


def fold(mine, other, out):
    out[...] = (mine[...] + other[...].astype(F32)).reshape(64, SLOTS, D).astype(BF)


def patch_back(dispatch, slots, score_grad, keys, out):
    dispatch.fetch()
    score_grad.fetch()
    keys.fetch()
    total = dot(dispatch.get().astype(BF), slots[...])
    out.put((total + dot(score_grad.get(), keys.get())).astype(BF))


def swap(value, axis):
    return lax.ppermute(value, axis, [(0, 1), (1, 0)])


def hop(value, flips):
    return lax.ppermute(value, ("dp", "yl"), [(at, at ^ flips) for at in range(4)])


NEXT, ACROSS, AROUND = 1, 2, 3


def exchange(value, axes):
    return lax.all_to_all(value, axes, split_axis=0, concat_axis=0, tiled=True)


def route(rows):
    return exchange(rows.reshape(64, 2 * SLOTS, D), ROUTE)


def local(patches, slot_keys, expert_in, expert_out, out_grad):
    first, second = expert_in[0], expert_out[0]
    half = first.shape[1]
    steps = half // TILE
    place = jnp.stack([lax.axis_index("core"), lax.axis_index("yl")]).astype(jnp.int32)
    place = (place, FLAG)
    block, full, final = ((256, D), BF), ((512, D), BF), ((256, D), F32)
    share = Out((256, 512), F32, room=True)

    own = exchange(jnp.broadcast_to(slot_keys[None], (64, SLOTS, D)), PLANE)
    rows, dispatch, keys = call(
        front, "front", 3, [Out(*full), share, Out(*full, room=True)],
        place, In(patches), own, swap(own, "core"),
    )
    rows = route(rows)
    grads, combine = call(
        front_grads, "front_grads", 2, [Out(*full), share], In(patches), In(keys, 512), In(out_grad)
    )
    grads = route(grads)

    def inward(routed, *after):
        return call(part_ways, "part_ways", 1, [block, block], place, routed, *after)

    def weights(after):
        return pl.pallas_call(
            lambda first, second, after, *refs: load(first, second, *refs),
            name="load",
            out_shape=[jax.ShapeDtypeStruct(value.shape, BF) for value in (first, second)],
            in_specs=[THERE] * 3,
            out_specs=[HERE] * 2,
            scratch_shapes=[pltpu.SemaphoreType.DMA((2,))],
            compiler_params=pltpu.CompilerParams(vmem_limit_bytes=LIMIT),
            cost_estimate=pl.CostEstimate(flops=2 * MICRO, bytes_accessed=1000, transcendentals=0),
        )(first, second, after)

    act_cuts, kept_cuts = [(0, D)], [(0, D)]
    for step in range(steps):
        at = D + 2 * TILE * step
        act_cuts += [(at, at + TILE), (at + TILE, at + 2 * TILE)]
        kept_cuts += [(D + TILE * step, D + TILE * (step + 1))]

    def ahead(name, blocks, outs, first, second, *after):
        rows = 256 * len(blocks)
        acts = Out((rows, D + 2 * half), BF, act_cuts, room=True)
        return call(forward, name, 2 * len(blocks), outs + [acts], *blocks, first, second, *after)

    def back(name, blocks, outs, first, second, acts, *after):
        rows = 256 * len(blocks)
        kept = Out((rows, D + half), BF, kept_cuts, room=True)
        slope = In(acts, rows, act_cuts)
        return call(backward, name, 2 * len(blocks), outs + [kept], *blocks, first, second, slope, *after)

    def join_up(name, ours, across, near, around, *after):
        (out,) = call(
            join, name, 2, [((64, 2 * SLOTS, D), BF)],
            place, ours, hop(across, ACROSS), hop(near, NEXT), hop(around, AROUND), *after,
        )
        return out

    ours, theirs = inward(rows)
    here = weights(theirs)
    ours_out, acts_ours = ahead("forward_ours", [ours], [final], *here)
    near_out, around_out, acts_near = ahead(
        "forward_near", [hop(theirs, NEXT), hop(theirs, AROUND)], [block, block], *here, After(acts_ours)
    )
    across_out, acts_across = ahead(
        "forward_across", [hop(ours, ACROSS)], [block], *here, After(acts_near)
    )

    ours, theirs = inward(grads, After(acts_across))
    near, around, across = hop(theirs, NEXT), hop(theirs, AROUND), hop(ours, ACROSS)
    ours_in, kept_ours = back("backward_ours", [ours], [final], *here, acts_ours)
    out = join_up("join_out", ours_out, across_out, near_out, around_out, After(kept_ours))
    slot_output = route(out).reshape(512, D)
    here = weights(out)
    near_in, around_in, kept_near = back(
        "backward_near", [near, around], [block, block], *here, acts_near
    )
    across_in, kept_across = back(
        "backward_across", [across], [block], *here, acts_across, After(kept_near)
    )
    into = join_up("join_in", ours_in, across_in, near_in, around_in)
    slot_in_grad = route(into).reshape(512, D)

    def weight_sum(name, towards, shape):
        pairs = ((acts_ours, kept_ours, 256), (acts_near, kept_near, 512), (acts_across, kept_across, 256))
        (out,) = call(
            lambda *refs: weight_grad(steps, towards, *refs), name, 4, [(shape, BF)],
            *[In(acts, rows, act_cuts) for acts, _, rows in pairs],
            *[In(kept, rows, kept_cuts) for _, kept, rows in pairs],
        )
        return out

    second_grad = weight_sum("second_grad", False, (half, D))
    first_grad = weight_sum("first_grad", True, (D, half))

    layer_out, mix = call(
        middle, "middle", 2, [Out(*block), share], slot_output, In(out_grad), In(combine, 256)
    )
    score_grad, kept, sent, _ = call(
        last, "last", 3, [Out((256, 512), BF, room=True), final, block, ((512, D), F32)],
        place, slot_in_grad, In(patches), In(dispatch, 256), In(mix, 256),
        After(first_grad), After(second_grad),
    )
    (folded,) = call(fold, "fold", 1, [((64, SLOTS, D), BF)], kept, swap(sent, "core"))
    own_total = jnp.sum(exchange(folded, PLANE).astype(F32), axis=0)
    (patch_grad,) = call(
        patch_back, "patch_back", 2, [Out(*block)],
        In(dispatch, 256), slot_in_grad, In(score_grad, 256), In(keys, 512),
    )
    own_total, patch_grad = lax.optimization_barrier((own_total, patch_grad))
    slot_key_grad = own_total + swap(own_total, "dp")
    return layer_out, patch_grad, slot_key_grad, first_grad[None], second_grad[None]


def solution(mesh):
    fine = Mesh(mesh.devices.reshape(2, 2, 8, 4, 2), TOKEN)
    return jax.shard_map(
        local,
        mesh=fine,
        in_specs=(
            P(TOKEN, None),
            P(EXPERT, None),
            P(EXPERT, None, "dp"),
            P(EXPERT, "dp", None),
            P(TOKEN, None),
        ),
        out_specs=(
            P(TOKEN, None),
            P(TOKEN, None),
            P(EXPERT, None),
            P(EXPERT, None, "dp"),
            P(EXPERT, "dp", None),
        ),
        check_vma=False,
    )
```

```python
import jax
import jax.numpy as jnp
from jax import lax
from jax.experimental import pallas as pl
from jax.experimental.pallas import tpu as pltpu
from jax.sharding import Mesh, PartitionSpec as P

D = 768
SLOTS = 4
BF = jnp.bfloat16
F32 = jnp.float32
EXPERT = ("yl", "z", "x", "core")
TOKEN = ("dp",) + EXPERT
ROUTE = ("core", "z", "x")
PLANE = ("z", "x", "yl")
TILE = 256
WIDE, TIGHT = 46 * 1024 * 1024, 52 * 1024 * 1024
SPARE = 8000000
MICRO = 1000000000
CUBIC = 0.044715
ROOT = 0.7978845608028654


def mm(left, right, contract):
    return lax.dot_general(left, right, (contract, ((), ())), preferred_element_type=F32)


def dot(left, right):
    return mm(left, right, ((1,), (0,)))


def dot_rows(left, right):
    return mm(left, right, ((0,), (0,)))


def dot_last(left, right):
    return mm(left, right, ((1,), (1,)))


class Far:
    def __init__(self, there, here, sems, first_sem, cuts, by_rows, start):
        self.there, self.here, self.sems, self.first_sem = there, here, sems, first_sem
        self.cuts, self.by_rows, self.start = cuts, by_rows, start

    def copy(self, piece, out):
        rows, cols = self.here.shape
        start, stop = self.cuts[piece] if self.cuts else (0, cols)
        at = (pl.ds(0, rows), pl.ds(start, stop - start))
        if self.by_rows:
            at = (pl.ds(start, stop - start), pl.ds(0, cols))
        near = self.here.at[at]
        far = self.there.at[at[0], pl.ds(self.start + start, stop - start)] if self.start else self.there.at[at]
        source, target = (near, far) if out else (far, near)
        return pltpu.make_async_copy(source, target, self.sems.at[self.first_sem + piece])

    def fetch(self, *pieces):
        for piece in pieces or (0,):
            self.copy(piece, False).start()

    def get(self, piece=0):
        self.copy(piece, False).wait()
        start, stop = self.cuts[piece] if self.cuts else (0, self.here.shape[1])
        return self.here[:, start:stop]

    def put(self, value, piece=0):
        start, stop = self.cuts[piece] if self.cuts else (0, self.here.shape[1])
        self.here[:, start:stop] = value
        self.copy(piece, True).start()

    def wait(self):
        for piece in range(len(self.cuts or (0,))):
            self.copy(piece, True).wait()


HERE = pl.BlockSpec(memory_space=pltpu.VMEM)
FLAG = pl.BlockSpec(memory_space=pltpu.SMEM)
THERE = pl.BlockSpec(memory_space=pl.ANY)


class In:
    def __init__(self, value, rows=None, cuts=None, by_rows=False, start=0, width=None):
        self.value, self.cuts, self.by_rows, self.start = value, cuts, by_rows, start
        self.shape = (rows or value.shape[0], width or value.shape[1])


class After:
    def __init__(self, value):
        self.value = value


class Out:
    def __init__(self, shape, dtype, cuts=None, room=False, by_rows=False):
        self.shape, self.dtype, self.cuts, self.by_rows = shape, dtype, cuts, by_rows
        width = shape[1] * jnp.dtype(dtype).itemsize
        self.rows = max(shape[0], -(-SPARE // width) // 256 * 256 + 256) if room else shape[0]


def call(kernel, name, cost, outs, *operands, limit=WIDE):
    values, specs, scratch, plan, sems = [], [], [], [], 0

    def far(shape, dtype, cuts, by_rows, start=0):
        nonlocal sems
        scratch.append(pltpu.VMEM(shape, dtype))
        sems += len(cuts or (0,))
        return len(scratch) - 1, sems - len(cuts or (0,)), cuts, by_rows, start

    for operand in operands:
        if isinstance(operand, In):
            values.append(operand.value)
            specs.append(THERE)
            plan.append(far(operand.shape, operand.value.dtype, operand.cuts, operand.by_rows, operand.start))
        elif isinstance(operand, After):
            values.append(operand.value)
            specs.append(THERE)
            plan.append(None)
        else:
            value, spec = operand if isinstance(operand, tuple) else (operand, HERE)
            values.append(value)
            specs.append(spec)
            plan.append(())
    shapes, out_specs = [], []
    for out in outs:
        if isinstance(out, Out):
            shapes.append(jax.ShapeDtypeStruct((out.rows, out.shape[1]), out.dtype))
            out_specs.append(THERE)
            plan.append(far(out.shape, out.dtype, out.cuts, out.by_rows))
        else:
            shapes.append(jax.ShapeDtypeStruct(*out))
            out_specs.append(HERE)
            plan.append(())

    def run(*refs):
        inner, waiting = [], []
        mine = refs[len(values) + len(outs) :]
        for at, (ref, how) in enumerate(zip(refs, plan)):
            if how is None:
                continue
            if how == ():
                inner.append(ref)
                continue
            inner.append(Far(ref, mine[how[0]], mine[-1], *how[1:]))
            if at >= len(values):
                waiting.append(inner[-1])
        kernel(*inner)
        for one in waiting:
            one.wait()

    return pl.pallas_call(
        run,
        name=name,
        out_shape=shapes,
        in_specs=specs,
        out_specs=out_specs,
        scratch_shapes=scratch + ([pltpu.SemaphoreType.DMA((sems,))] if sems else []),
        compiler_params=pltpu.CompilerParams(vmem_limit_bytes=limit),
        cost_estimate=pl.CostEstimate(flops=cost * MICRO, bytes_accessed=1000, transcendentals=0),
    )(*values)


def flat(ref):
    value = ref[...].astype(F32)
    return value.reshape(value.shape[0] * value.shape[1], D).astype(BF)


def split(value, yl):
    low, high = value[:, :SLOTS, :], value[:, SLOTS:, :]
    rows = value.shape[0] * SLOTS
    ours = jnp.where(yl == 0, low, high).reshape(rows, D)
    theirs = jnp.where(yl == 0, high, low).reshape(rows, D)
    return ours, theirs


def merge(ours, theirs, yl):
    groups = (ours.shape[0] // SLOTS, SLOTS, D)
    ours, theirs = ours.reshape(groups), theirs.reshape(groups)
    low, high = jnp.where(yl == 0, ours, theirs), jnp.where(yl == 0, theirs, ours)
    return jnp.concatenate([low, high], axis=1)


def softmax(scores, axis):
    raised = jnp.exp(scores - jnp.max(scores, axis=axis, keepdims=True))
    return raised / jnp.sum(raised, axis=axis, keepdims=True)


def softmax_back(share, share_grad, axis):
    return share * (share_grad - jnp.sum(share_grad * share, axis=axis, keepdims=True))


def front(place, patches, own, other, rows, dispatch, keys):
    patches.fetch()
    core = place[0]
    for at, block in ((core, own), (1 - core, other)):
        keys.here[pl.ds(pl.multiple_of(at * 256, 256), 256), :] = flat(block)
    keys.copy(0, True).start()
    image = patches.get()
    share = softmax(dot_last(image, keys.here[...]), 0)
    dispatch.put(share)
    rows.put(dot_rows(share.astype(BF), image).astype(BF))


def front_grads(patches, keys, out_grad, grads, combine):
    patches.fetch()
    keys.fetch()
    out_grad.fetch()
    share = softmax(dot_last(patches.get(), keys.get()), 1)
    combine.put(share)
    grads.put(dot_rows(share.astype(BF), out_grad.get()).astype(BF))


def part_ways(place, routed, ours, theirs):
    near, far = split(routed[...].astype(F32), place[1])
    ours[...] = near.astype(BF)
    theirs[...] = far.astype(BF)


def begin(*fars):
    for piece in range(2):
        for far in fars:
            far.fetch(piece)


def arrived(step, *fars):
    if step < 2:
        for far in fars:
            far.copy(step, False).wait()


def load(first, second, first_here, second_here, sems):
    copies = [
        pltpu.make_async_copy(first, first_here, sems.at[0]),
        pltpu.make_async_copy(second, second_here, sems.at[1]),
    ]
    for copy in copies:
        copy.start()
    for copy in copies:
        copy.wait()


def forward(*refs):
    blocks = (len(refs) - 3) // 2
    low, first, second, outs, acts = refs[:blocks], *refs[blocks : blocks + 2], refs[-blocks - 1 : -1], refs[-1]
    here = jnp.concatenate([ref[...] for ref in low], axis=0)
    acts.put(here, 0)
    total = None
    for step in range(first.shape[1] // TILE):
        part = slice(step * TILE, step * TILE + TILE)
        value = dot(here, first[:, part])
        square = value * value
        bend = jnp.tanh(ROOT * value * (1.0 + CUBIC * square))
        gate = 0.5 + 0.5 * bend
        active = (value * gate).astype(BF)
        acts.put(active, 1 + step)
        rise = (0.5 * ROOT) * value * (1.0 - bend * bend) * (1.0 + (3.0 * CUBIC) * square)
        acts.put((gate + rise).astype(BF), 1 + first.shape[1] // TILE + step)
        term = dot(active, second[part, :])
        total = term if total is None else total + term
    for at, out in enumerate(outs):
        out[...] = total[at * 256 : at * 256 + 256].astype(out.dtype)


def backward(*refs):
    blocks = (len(refs) - 4) // 2
    low, first, second, slope, outs, kept = (
        refs[:blocks], *refs[blocks : blocks + 3], refs[-blocks - 1 : -1], refs[-1],
    )
    far = [one for one in (second, slope, first) if isinstance(one, Far)]
    begin(*far)
    first, second = (one.here if isinstance(one, Far) else one for one in (first, second))
    here = jnp.concatenate([ref[...] for ref in low], axis=0)
    kept.put(here, 0)
    total = None
    for step in range(first.shape[1] // TILE):
        arrived(step, *far)
        part = slice(step * TILE, step * TILE + TILE)
        rounded = (dot_last(here, second[part, :]) * slope.here[:, part].astype(F32)).astype(BF)
        kept.put(rounded, 1 + step)
        term = dot_last(rounded, first[:, part])
        total = term if total is None else total + term
    for at, out in enumerate(outs):
        out[...] = total[at * 256 : at * 256 + 256].astype(out.dtype)


def weight_grad(steps, into, *refs):
    acts, kept, out, done = refs[:3], refs[3:6], refs[6], refs[7]
    done[...] = jnp.zeros((8, 128), F32)
    narrow = [1 + step for step in range(steps)] if not into else [0]
    other = [0] if not into else [1 + step for step in range(steps)]
    for step in range(steps):
        for act, keep in zip(acts, kept):
            if step == 0 or not into:
                act.fetch(narrow[0 if into else step])
            if step == 0 or into:
                keep.fetch(other[step if into else 0])
    held = [(keep if not into else act).get(0) for act, keep in zip(acts, kept)]
    for step in range(steps):
        part = slice(step * TILE, step * TILE + TILE)
        total = None
        for act, keep, one in zip(acts, kept, held):
            moving = keep.get(other[step]) if into else act.get(narrow[step])
            term = dot_rows(one, moving) if into else dot_rows(moving, one)
            total = term if total is None else total + term
        if into:
            out[:, part] = total.astype(BF)
        else:
            out[part, :] = total.astype(BF)


def join(place, ours, ours_far, theirs, theirs_far, out):
    near = ours[...] + ours_far[...].astype(F32)
    far = theirs[...].astype(F32) + theirs_far[...].astype(F32)
    out[...] = merge(near, far, place[1]).astype(BF)


def middle(slot_output, out_grad, combine, layer_out, mix):
    out_grad.fetch()
    combine.fetch()
    grad = dot_last(out_grad.get(), slot_output[...])
    share = combine.get()
    mix.put(softmax_back(share, grad, 1))
    layer_out.put(dot(share.astype(BF), slot_output[...]).astype(BF))


def last(place, slot_in_grad, patches, dispatch, mix, score_grad, kept, sent, term):
    patches.fetch()
    dispatch.fetch()
    mix.fetch()
    image = patches.get()
    grad = dot_last(image, slot_in_grad[...])
    change = softmax_back(dispatch.get(), grad, 0)
    score = (mix.get() + change).astype(BF)
    score_grad.put(score)
    term[...] = dot_rows(score, image)
    core = place[0]
    kept[...] = term[pl.ds(pl.multiple_of(core * 256, 256), 256), :]
    sent[...] = term[pl.ds(pl.multiple_of((1 - core) * 256, 256), 256), :].astype(BF)


def fold(mine, other, out):
    out[...] = (mine[...] + other[...].astype(F32)).reshape(64, SLOTS, D).astype(BF)


def patch_back(dispatch, slots, score_grad, keys, out):
    dispatch.fetch()
    score_grad.fetch()
    keys.fetch()
    total = dot(dispatch.get().astype(BF), slots[...])
    out.put((total + dot(score_grad.get(), keys.get())).astype(BF))


def swap(value, axis):
    return lax.ppermute(value, axis, [(0, 1), (1, 0)])


def hop(value, flips):
    return lax.ppermute(value, ("dp", "yl"), [(at, at ^ flips) for at in range(4)])


NEXT, ACROSS, AROUND = 1, 2, 3


def exchange(value, axes):
    return lax.all_to_all(value, axes, split_axis=0, concat_axis=0, tiled=True)


def route(rows):
    return exchange(rows.reshape(64, 2 * SLOTS, D), ROUTE)


def local(patches, slot_keys, expert_in, expert_out, out_grad):
    first, second = expert_in[0], expert_out[0]
    half = first.shape[1]
    steps = half // TILE
    place = jnp.stack([lax.axis_index("core"), lax.axis_index("yl")]).astype(jnp.int32)
    place = (place, FLAG)
    block, full, final = ((256, D), BF), ((512, D), BF), ((256, D), F32)
    share = Out((256, 512), F32, room=True)

    own = exchange(jnp.broadcast_to(slot_keys[None], (64, SLOTS, D)), PLANE)
    rows, dispatch, keys = call(
        front, "front", 3, [Out(*full), share, Out(*full, room=True)],
        place, In(patches), own, swap(own, "core"),
    )
    rows = route(rows)
    grads, combine = call(
        front_grads, "front_grads", 2, [Out(*full), share], In(patches), In(keys, 512), In(out_grad)
    )
    early, grads = grads, route(grads)

    def inward(routed, *after):
        return call(part_ways, "part_ways", 1, [block, block], place, routed, *after)

    def weights(after):
        return pl.pallas_call(
            lambda first, second, after, *refs: load(first, second, *refs),
            name="load",
            out_shape=[jax.ShapeDtypeStruct(value.shape, BF) for value in (first, second)],
            in_specs=[THERE] * 3,
            out_specs=[HERE] * 2,
            scratch_shapes=[pltpu.SemaphoreType.DMA((2,))],
            compiler_params=pltpu.CompilerParams(vmem_limit_bytes=WIDE),
            cost_estimate=pl.CostEstimate(flops=1000, bytes_accessed=1000, transcendentals=0),
        )(first, second, after)

    act_cuts, kept_cuts = [(0, D)], [(0, D)]
    for step in range(2 * steps):
        act_cuts += [(D + TILE * step, D + TILE * (step + 1))]
    kept_cuts += act_cuts[1 : 1 + steps]
    slope_at = D + half
    pieces = [(0, TILE), (TILE, half)]
    fetched = In(first, cuts=pieces), In(second, cuts=pieces, by_rows=True)

    def ahead(name, blocks, outs, *after):
        rows = 256 * len(blocks)
        acts = Out((rows, D + 2 * half), BF, act_cuts, room=True)
        return call(forward, name, 60 if name == "forward_across" else 0, outs + [acts], *blocks, *here, *after, limit=WIDE)

    def back(name, blocks, outs, weights, acts, *after):
        rows = 256 * len(blocks)
        kept = Out((rows, D + half), BF, kept_cuts, room=True)
        slope = In(acts, rows, pieces, start=slope_at, width=half)
        cost, limit = (10, WIDE) if weights is here else (30, TIGHT)
        return call(backward, name, cost, outs + [kept], *blocks, *weights, slope, *after, limit=limit)

    def join_up(name, ours, across, near, around, *after):
        (out,) = call(
            join, name, 20, [((64, 2 * SLOTS, D), BF)],
            place, ours, hop(across, ACROSS), hop(near, NEXT), hop(around, AROUND), *after,
        )
        return out

    ours, theirs = inward(rows, After(early))
    here = weights(theirs)
    near_out, around_out, acts_near = ahead(
        "forward_near", [hop(theirs, NEXT), hop(theirs, AROUND)], [block, block]
    )
    across_out, acts_across = ahead(
        "forward_across", [hop(ours, ACROSS)], [block], After(acts_near)
    )
    ours_out, acts_ours = ahead("forward_ours", [ours], [final], After(acts_across))

    ours, theirs = inward(grads, After(acts_ours))
    near, around, across = hop(theirs, NEXT), hop(theirs, AROUND), hop(ours, ACROSS)
    ours_in, kept_ours = back("backward_ours", [ours], [final], here, acts_ours)
    out = join_up("join_out", ours_out, across_out, near_out, around_out, After(kept_ours))
    slot_output = route(out).reshape(512, D)
    near_in, around_in, kept_near = back(
        "backward_near", [near, around], [block, block], fetched, acts_near, After(out)
    )
    across_in, kept_across = back(
        "backward_across", [across], [block], fetched, acts_across, After(kept_near)
    )
    into = join_up("join_in", ours_in, across_in, near_in, around_in, After(slot_output))
    slot_in_grad = route(into).reshape(512, D)

    def weight_sum(name, towards, shape):
        pairs = ((acts_ours, kept_ours, 256), (acts_near, kept_near, 512), (acts_across, kept_across, 256))
        return call(
            lambda *refs: weight_grad(steps, towards, *refs), name, 4, [(shape, BF), ((8, 128), F32)],
            *[In(acts, rows, act_cuts) for acts, _, rows in pairs],
            *[In(kept, rows, kept_cuts) for _, kept, rows in pairs],
        )

    second_grad, second_done = weight_sum("second_grad", False, (half, D))
    first_grad, first_done = weight_sum("first_grad", True, (D, half))

    layer_out, mix = call(
        middle, "middle", 2, [Out(*block), share], slot_output, In(out_grad), In(combine, 256)
    )
    score_grad, kept, sent, _ = call(
        last, "last", 3, [Out((256, 512), BF, room=True), final, block, ((512, D), F32)],
        place, slot_in_grad, In(patches), In(dispatch, 256), In(mix, 256),
        After(first_done), After(second_done),
    )
    (folded,) = call(fold, "fold", 1, [((64, SLOTS, D), BF)], kept, swap(sent, "core"))
    own_total = jnp.sum(exchange(folded, PLANE).astype(F32), axis=0)
    (patch_grad,) = call(
        patch_back, "patch_back", 2, [Out(*block)],
        In(dispatch, 256), slot_in_grad, In(score_grad, 256), In(keys, 512),
    )
    own_total, patch_grad = lax.optimization_barrier((own_total, patch_grad))
    slot_key_grad = own_total + swap(own_total, "dp")
    return layer_out, patch_grad, slot_key_grad, first_grad[None], second_grad[None]


def solution(mesh):
    fine = Mesh(mesh.devices.reshape(2, 2, 8, 4, 2), TOKEN)
    return jax.shard_map(
        local,
        mesh=fine,
        in_specs=(
            P(TOKEN, None),
            P(EXPERT, None),
            P(EXPERT, None, "dp"),
            P(EXPERT, "dp", None),
            P(TOKEN, None),
        ),
        out_specs=(
            P(TOKEN, None),
            P(TOKEN, None),
            P(EXPERT, None),
            P(EXPERT, None, "dp"),
            P(EXPERT, "dp", None),
        ),
        check_vma=False,
    )
```

```python
import jax
import jax.numpy as jnp
from jax import lax
from jax.experimental import pallas as pl
from jax.experimental.pallas import tpu as pltpu
from jax.sharding import Mesh, PartitionSpec as P

D = 768
SLOTS = 4
BF = jnp.bfloat16
F32 = jnp.float32
EXPERT = ("yl", "z", "x", "core")
TOKEN = ("dp",) + EXPERT
ROUTE = ("core", "z", "x")
PLANE = ("z", "x", "yl")
TILE = 256
WIDE, TIGHT = 46 * 1024 * 1024, 52 * 1024 * 1024
SPARE = 8000000
MICRO = 1000000000
CUBIC = 0.044715
ROOT = 0.7978845608028654


def mm(left, right, contract):
    return lax.dot_general(left, right, (contract, ((), ())), preferred_element_type=F32)


def dot(left, right):
    return mm(left, right, ((1,), (0,)))


def dot_rows(left, right):
    return mm(left, right, ((0,), (0,)))


def dot_last(left, right):
    return mm(left, right, ((1,), (1,)))


class Far:
    def __init__(self, there, here, sems, first_sem, cuts, by_rows, start):
        self.there, self.here, self.sems, self.first_sem = there, here, sems, first_sem
        self.cuts, self.by_rows, self.start = cuts, by_rows, start

    def copy(self, piece, out):
        rows, cols = self.here.shape
        start, stop = self.cuts[piece] if self.cuts else (0, cols)
        at = (pl.ds(0, rows), pl.ds(start, stop - start))
        if self.by_rows:
            at = (pl.ds(start, stop - start), pl.ds(0, cols))
        near = self.here.at[at]
        far = self.there.at[at[0], pl.ds(self.start + start, stop - start)] if self.start else self.there.at[at]
        source, target = (near, far) if out else (far, near)
        return pltpu.make_async_copy(source, target, self.sems.at[self.first_sem + piece])

    def fetch(self, *pieces):
        for piece in pieces or (0,):
            self.copy(piece, False).start()

    def get(self, piece=0):
        self.copy(piece, False).wait()
        start, stop = self.cuts[piece] if self.cuts else (0, self.here.shape[1])
        return self.here[:, start:stop]

    def put(self, value, piece=0):
        start, stop = self.cuts[piece] if self.cuts else (0, self.here.shape[1])
        self.here[:, start:stop] = value
        self.copy(piece, True).start()

    def wait(self):
        for piece in range(len(self.cuts or (0,))):
            self.copy(piece, True).wait()


HERE = pl.BlockSpec(memory_space=pltpu.VMEM)
FLAG = pl.BlockSpec(memory_space=pltpu.SMEM)
THERE = pl.BlockSpec(memory_space=pl.ANY)


class In:
    def __init__(self, value, rows=None, cuts=None, by_rows=False, start=0, width=None):
        self.value, self.cuts, self.by_rows, self.start = value, cuts, by_rows, start
        self.shape = (rows or value.shape[0], width or value.shape[1])


class After:
    def __init__(self, value):
        self.value = value


class Out:
    def __init__(self, shape, dtype, cuts=None, room=False, by_rows=False):
        self.shape, self.dtype, self.cuts, self.by_rows = shape, dtype, cuts, by_rows
        width = shape[1] * jnp.dtype(dtype).itemsize
        self.rows = max(shape[0], -(-SPARE // width) // 256 * 256 + 256) if room else shape[0]


def call(kernel, name, cost, outs, *operands, limit=WIDE, extra=()):
    values, specs, scratch, plan, sems = [], [], [], [], 0

    def far(shape, dtype, cuts, by_rows, start=0):
        nonlocal sems
        scratch.append(pltpu.VMEM(shape, dtype))
        sems += len(cuts or (0,))
        return len(scratch) - 1, sems - len(cuts or (0,)), cuts, by_rows, start

    for operand in operands:
        if isinstance(operand, In):
            values.append(operand.value)
            specs.append(THERE)
            plan.append(far(operand.shape, operand.value.dtype, operand.cuts, operand.by_rows, operand.start))
        elif isinstance(operand, After):
            values.append(operand.value)
            specs.append(THERE)
            plan.append(None)
        else:
            value, spec = operand if isinstance(operand, tuple) else (operand, HERE)
            values.append(value)
            specs.append(spec)
            plan.append(())
    shapes, out_specs = [], []
    for out in outs:
        if isinstance(out, Out):
            shapes.append(jax.ShapeDtypeStruct((out.rows, out.shape[1]), out.dtype))
            out_specs.append(THERE)
            plan.append(far(out.shape, out.dtype, out.cuts, out.by_rows))
        else:
            shapes.append(jax.ShapeDtypeStruct(*out))
            out_specs.append(HERE)
            plan.append(())

    def run(*refs):
        inner, waiting = [], []
        mine = refs[len(values) + len(outs) :]
        for at, (ref, how) in enumerate(zip(refs, plan)):
            if how is None:
                continue
            if how == ():
                inner.append(ref)
                continue
            inner.append(Far(ref, mine[how[0]], mine[-1], *how[1:]))
            if at >= len(values):
                waiting.append(inner[-1])
        kernel(*inner, *mine[len(scratch) : len(scratch) + len(extra)])
        for one in waiting:
            one.wait()

    return pl.pallas_call(
        run,
        name=name,
        out_shape=shapes,
        in_specs=specs,
        out_specs=out_specs,
        scratch_shapes=scratch + list(extra) + ([pltpu.SemaphoreType.DMA((sems,))] if sems else []),
        compiler_params=pltpu.CompilerParams(vmem_limit_bytes=limit),
        cost_estimate=pl.CostEstimate(flops=cost * MICRO, bytes_accessed=1000, transcendentals=0),
    )(*values)


def flat(ref):
    value = ref[...].astype(F32)
    return value.reshape(value.shape[0] * value.shape[1], D).astype(BF)


def split(value, yl):
    low, high = value[:, :SLOTS, :], value[:, SLOTS:, :]
    rows = value.shape[0] * SLOTS
    ours = jnp.where(yl == 0, low, high).reshape(rows, D)
    theirs = jnp.where(yl == 0, high, low).reshape(rows, D)
    return ours, theirs


def merge(ours, theirs, yl):
    groups = (ours.shape[0] // SLOTS, SLOTS, D)
    ours, theirs = ours.reshape(groups), theirs.reshape(groups)
    low, high = jnp.where(yl == 0, ours, theirs), jnp.where(yl == 0, theirs, ours)
    return jnp.concatenate([low, high], axis=1)


def softmax(scores, axis):
    raised = jnp.exp(scores - jnp.max(scores, axis=axis, keepdims=True))
    return raised / jnp.sum(raised, axis=axis, keepdims=True)


def softmax_back(share, share_grad, axis):
    return share * (share_grad - jnp.sum(share_grad * share, axis=axis, keepdims=True))


def front(place, patches, own, other, rows, dispatch, keys):
    patches.fetch()
    core = place[0]
    for at, block in ((core, own), (1 - core, other)):
        keys.here[pl.ds(pl.multiple_of(at * 256, 256), 256), :] = flat(block)
    keys.copy(0, True).start()
    image = patches.get()
    share = softmax(dot_last(image, keys.here[...]), 0)
    dispatch.put(share)
    rows.put(dot_rows(share.astype(BF), image).astype(BF))


def front_grads(patches, keys, out_grad, grads, combine):
    patches.fetch()
    keys.fetch()
    out_grad.fetch()
    share = softmax(dot_last(patches.get(), keys.get()), 1)
    combine.put(share)
    grads.put(dot_rows(share.astype(BF), out_grad.get()).astype(BF))


def part_ways(place, routed, ours, theirs):
    near, far = split(routed[...].astype(F32), place[1])
    ours[...] = near.astype(BF)
    theirs[...] = far.astype(BF)


def begin(*fars):
    for piece in range(2):
        for far in fars:
            far.fetch(piece)


def arrived(step, *fars):
    if step < 2:
        for far in fars:
            far.copy(step, False).wait()


def forward(*refs):
    blocks = (len(refs) - 3) // 2
    low, first, second, outs, acts = refs[:blocks], *refs[blocks : blocks + 2], refs[-blocks - 1 : -1], refs[-1]
    begin(first, second)
    here = jnp.concatenate([ref[...] for ref in low], axis=0)
    acts.put(here, 0)
    total = None
    for step in range(first.here.shape[1] // TILE):
        arrived(step, first)
        part = slice(step * TILE, step * TILE + TILE)
        value = dot(here, first.here[:, part])
        square = value * value
        bend = jnp.tanh(ROOT * value * (1.0 + CUBIC * square))
        gate = 0.5 + 0.5 * bend
        active = (value * gate).astype(BF)
        acts.put(active, 1 + step)
        rise = (0.5 * ROOT) * value * (1.0 - bend * bend) * (1.0 + (3.0 * CUBIC) * square)
        acts.put((gate + rise).astype(BF), 1 + first.here.shape[1] // TILE + step)
        arrived(step, second)
        term = dot(active, second.here[part, :])
        total = term if total is None else total + term
    for at, out in enumerate(outs):
        out[...] = total[at * 256 : at * 256 + 256].astype(out.dtype)


def backward(*refs):
    blocks = (len(refs) - 4) // 2
    low, first, second, slope, outs, kept = (
        refs[:blocks], *refs[blocks : blocks + 3], refs[-blocks - 1 : -1], refs[-1],
    )
    begin(second, slope, first)
    here = jnp.concatenate([ref[...] for ref in low], axis=0)
    kept.put(here, 0)
    total = None
    for step in range(first.here.shape[1] // TILE):
        arrived(step, second, slope)
        part = slice(step * TILE, step * TILE + TILE)
        rounded = (dot_last(here, second.here[part, :]) * slope.here[:, part].astype(F32)).astype(BF)
        kept.put(rounded, 1 + step)
        arrived(step, first)
        term = dot_last(rounded, first.here[:, part])
        total = term if total is None else total + term
    for at, out in enumerate(outs):
        out[...] = total[at * 256 : at * 256 + 256].astype(out.dtype)


def weight_grad(steps, into, *refs):
    acts, kept, out, done = refs[:3], refs[3:6], refs[6], refs[7]
    done[...] = jnp.zeros((8, 128), F32)
    narrow = [1 + step for step in range(steps)] if not into else [0]
    other = [0] if not into else [1 + step for step in range(steps)]
    for step in range(steps):
        for act, keep in zip(acts, kept):
            if step == 0 or not into:
                act.fetch(narrow[0 if into else step])
            if step == 0 or into:
                keep.fetch(other[step if into else 0])
    held = [(keep if not into else act).get(0) for act, keep in zip(acts, kept)]
    for step in range(steps):
        part = slice(step * TILE, step * TILE + TILE)
        total = None
        for act, keep, one in zip(acts, kept, held):
            moving = keep.get(other[step]) if into else act.get(narrow[step])
            term = dot_rows(one, moving) if into else dot_rows(moving, one)
            total = term if total is None else total + term
        if into:
            out[:, part] = total.astype(BF)
        else:
            out[part, :] = total.astype(BF)


def join(place, ours, ours_far, theirs, theirs_far, out):
    near = ours[...] + ours_far[...].astype(F32)
    far = theirs[...].astype(F32) + theirs_far[...].astype(F32)
    out[...] = merge(near, far, place[1]).astype(BF)


def middle(slot_output, out_grad, combine, layer_out, mix):
    out_grad.fetch()
    combine.fetch()
    grad = dot_last(out_grad.get(), slot_output[...])
    share = combine.get()
    mix.put(softmax_back(share, grad, 1))
    layer_out.put(dot(share.astype(BF), slot_output[...]).astype(BF))


def last(place, slot_in_grad, patches, dispatch, mix, score_grad, kept, sent, term):
    patches.fetch()
    dispatch.fetch()
    mix.fetch()
    image = patches.get()
    grad = dot_last(image, slot_in_grad[...])
    change = softmax_back(dispatch.get(), grad, 0)
    score = (mix.get() + change).astype(BF)
    score_grad.put(score)
    term[...] = dot_rows(score, image)
    core = place[0]
    kept[...] = term[pl.ds(pl.multiple_of(core * 256, 256), 256), :]
    sent[...] = term[pl.ds(pl.multiple_of((1 - core) * 256, 256), 256), :].astype(BF)


def fold(mine, other, out):
    out[...] = (mine[...] + other[...].astype(F32)).reshape(64, SLOTS, D).astype(BF)


def patch_back(dispatch, slots, score_grad, keys, out):
    dispatch.fetch()
    score_grad.fetch()
    keys.fetch()
    total = dot(dispatch.get().astype(BF), slots[...])
    out.put((total + dot(score_grad.get(), keys.get())).astype(BF))


def swap(value, axis):
    return lax.ppermute(value, axis, [(0, 1), (1, 0)])


def hop(value, flips):
    return lax.ppermute(value, ("dp", "yl"), [(at, at ^ flips) for at in range(4)])


NEXT, ACROSS, AROUND = 1, 2, 3


def exchange(value, axes):
    return lax.all_to_all(value, axes, split_axis=0, concat_axis=0, tiled=True)


def route(rows):
    return exchange(rows.reshape(64, 2 * SLOTS, D), ROUTE)


def local(patches, slot_keys, expert_in, expert_out, out_grad):
    first, second = expert_in[0], expert_out[0]
    half = first.shape[1]
    steps = half // TILE
    place = jnp.stack([lax.axis_index("core"), lax.axis_index("yl")]).astype(jnp.int32)
    place = (place, FLAG)
    block, full, final = ((256, D), BF), ((512, D), BF), ((256, D), F32)
    share = Out((256, 512), F32, room=True)

    own = exchange(jnp.broadcast_to(slot_keys[None], (64, SLOTS, D)), PLANE)
    rows, dispatch, keys = call(
        front, "front", 3, [Out(*full), share, Out(*full, room=True)],
        place, In(patches), own, swap(own, "core"),
    )
    rows = route(rows)
    grads, combine = call(
        front_grads, "front_grads", 2, [Out(*full), share], In(patches), In(keys, 512), In(out_grad)
    )
    early, grads = grads, route(grads)

    def inward(routed, *after):
        return call(part_ways, "part_ways", 1, [block, block], place, routed, *after)

    act_cuts, kept_cuts = [(0, D)], [(0, D)]
    for step in range(2 * steps):
        act_cuts += [(D + TILE * step, D + TILE * (step + 1))]
    kept_cuts += act_cuts[1 : 1 + steps]
    slope_at = D + half
    pieces = [(0, TILE), (TILE, half)]
    fetched = In(first, cuts=pieces), In(second, cuts=pieces, by_rows=True)

    def ahead(name, blocks, outs, *after):
        rows = 256 * len(blocks)
        acts = Out((rows, D + 2 * half), BF, act_cuts, room=True)
        return call(forward, name, 60 if name == "forward_across" else 0, outs + [acts], *blocks, *fetched, *after, limit=TIGHT)

    def back(name, blocks, outs, acts, *after):
        rows = 256 * len(blocks)
        kept = Out((rows, D + half), BF, kept_cuts, room=True)
        slope = In(acts, rows, pieces, start=slope_at, width=half)
        cost = 10 if name == "backward_ours" else 30
        return call(backward, name, cost, outs + [kept], *blocks, *fetched, slope, *after, limit=TIGHT)

    def outward(across, near, around):
        return hop(across, ACROSS), hop(near, NEXT), hop(around, AROUND)

    def join_up(name, *operands):
        return call(join, name, 20, [((64, 2 * SLOTS, D), BF)], place, *operands)[0]

    ours, theirs = inward(rows, After(early))
    near_out, around_out, acts_near = ahead(
        "forward_near", [hop(theirs, NEXT), hop(theirs, AROUND)], [block, block]
    )
    across_out, acts_across = ahead(
        "forward_across", [hop(ours, ACROSS)], [block], After(acts_near)
    )
    ours_out, acts_ours = ahead("forward_ours", [ours], [final], After(acts_across))

    ours, theirs = inward(grads, After(acts_ours))
    ours_in, kept_ours = back("backward_ours", [ours], [final], acts_ours)
    received = outward(across_out, near_out, around_out)
    ours, theirs, *received = lax.optimization_barrier((ours, theirs, *received))
    near, around, across = hop(theirs, NEXT), hop(theirs, AROUND), hop(ours, ACROSS)
    out = join_up("join_out", ours_out, *received, After(kept_ours))
    slot_output = route(out).reshape(512, D)
    near_in, around_in, kept_near = back(
        "backward_near", [near, around], [block, block], acts_near, After(out)
    )
    across_in, kept_across = back(
        "backward_across", [across], [block], acts_across, After(kept_near)
    )
    into = join_up("join_in", ours_in, *outward(across_in, near_in, around_in), After(slot_output))
    slot_in_grad = route(into).reshape(512, D)

    def weight_sum(name, towards, shape):
        pairs = ((acts_ours, kept_ours, 256), (acts_near, kept_near, 512), (acts_across, kept_across, 256))
        return call(
            lambda *refs: weight_grad(steps, towards, *refs), name, 4, [(shape, BF), ((8, 128), F32)],
            *[In(acts, rows, act_cuts) for acts, _, rows in pairs],
            *[In(kept, rows, kept_cuts) for _, kept, rows in pairs],
        )

    second_grad, second_done = weight_sum("second_grad", False, (half, D))
    first_grad, first_done = weight_sum("first_grad", True, (D, half))

    layer_out, mix = call(
        middle, "middle", 2, [Out(*block), share], slot_output, In(out_grad), In(combine, 256)
    )
    score_grad, kept, sent = call(
        last, "last", 3, [Out((256, 512), BF, room=True), final, block],
        place, slot_in_grad, In(patches), In(dispatch, 256), In(mix, 256),
        After(first_done), After(second_done), extra=(pltpu.VMEM((512, D), F32),),
    )
    (folded,) = call(fold, "fold", 1, [((64, SLOTS, D), BF)], kept, swap(sent, "core"))
    own_total = jnp.sum(exchange(folded, PLANE).astype(F32), axis=0)
    (patch_grad,) = call(
        patch_back, "patch_back", 2, [Out(*block)],
        In(dispatch, 256), slot_in_grad, In(score_grad, 256), In(keys, 512),
    )
    own_total, patch_grad = lax.optimization_barrier((own_total, patch_grad))
    slot_key_grad = own_total + swap(own_total, "dp")
    return layer_out, patch_grad, slot_key_grad, first_grad[None], second_grad[None]


def solution(mesh):
    fine = Mesh(mesh.devices.reshape(2, 2, 8, 4, 2), TOKEN)
    return jax.shard_map(
        local,
        mesh=fine,
        in_specs=(
            P(TOKEN, None),
            P(EXPERT, None),
            P(EXPERT, None, "dp"),
            P(EXPERT, "dp", None),
            P(TOKEN, None),
        ),
        out_specs=(
            P(TOKEN, None),
            P(TOKEN, None),
            P(EXPERT, None),
            P(EXPERT, None, "dp"),
            P(EXPERT, "dp", None),
        ),
        check_vma=False,
    )
```

```python
import jax
import jax.numpy as jnp
from jax import lax
from jax.experimental import pallas as pl
from jax.experimental.pallas import tpu as pltpu
from jax.sharding import Mesh, PartitionSpec as P

D = 768
SLOTS = 4
BF = jnp.bfloat16
F32 = jnp.float32
EXPERT = ("yl", "z", "x", "core")
TOKEN = ("dp",) + EXPERT
ROUTE = ("core", "z", "x")
PLANE = ("z", "x", "yl")
TILE = 256
WIDE, TIGHT = 46 * 1024 * 1024, 52 * 1024 * 1024
SPARE = 8000000
MICRO = 1000000000
CUBIC = 0.044715
ROOT = 0.7978845608028654


def mm(left, right, contract):
    return lax.dot_general(left, right, (contract, ((), ())), preferred_element_type=F32)


def dot(left, right):
    return mm(left, right, ((1,), (0,)))


def dot_rows(left, right):
    return mm(left, right, ((0,), (0,)))


def dot_last(left, right):
    return mm(left, right, ((1,), (1,)))


class Far:
    def __init__(self, there, here, sems, first_sem, cuts, by_rows, start):
        self.there, self.here, self.sems, self.first_sem = there, here, sems, first_sem
        self.cuts, self.by_rows, self.start = cuts, by_rows, start

    def copy(self, piece, out):
        rows, cols = self.here.shape
        start, stop = self.cuts[piece] if self.cuts else (0, cols)
        at = (pl.ds(0, rows), pl.ds(start, stop - start))
        if self.by_rows:
            at = (pl.ds(start, stop - start), pl.ds(0, cols))
        near = self.here.at[at]
        far = self.there.at[at[0], pl.ds(self.start + start, stop - start)] if self.start else self.there.at[at]
        source, target = (near, far) if out else (far, near)
        return pltpu.make_async_copy(source, target, self.sems.at[self.first_sem + piece])

    def fetch(self, *pieces):
        for piece in pieces or (0,):
            self.copy(piece, False).start()

    def get(self, piece=0):
        self.copy(piece, False).wait()
        start, stop = self.cuts[piece] if self.cuts else (0, self.here.shape[1])
        return self.here[:, start:stop]

    def put(self, value, piece=0):
        start, stop = self.cuts[piece] if self.cuts else (0, self.here.shape[1])
        self.here[:, start:stop] = value
        self.copy(piece, True).start()

    def wait(self):
        for piece in range(len(self.cuts or (0,))):
            self.copy(piece, True).wait()


HERE = pl.BlockSpec(memory_space=pltpu.VMEM)
FLAG = pl.BlockSpec(memory_space=pltpu.SMEM)
THERE = pl.BlockSpec(memory_space=pl.ANY)


class In:
    def __init__(self, value, rows=None, cuts=None, by_rows=False, start=0, width=None):
        self.value, self.cuts, self.by_rows, self.start = value, cuts, by_rows, start
        self.shape = (rows or value.shape[0], width or value.shape[1])


class After:
    def __init__(self, value):
        self.value = value


class Out:
    def __init__(self, shape, dtype, cuts=None, room=False, by_rows=False):
        self.shape, self.dtype, self.cuts, self.by_rows = shape, dtype, cuts, by_rows
        width = shape[1] * jnp.dtype(dtype).itemsize
        self.rows = max(shape[0], -(-SPARE // width) // 256 * 256 + 256) if room else shape[0]


def call(kernel, name, cost, outs, *operands, limit=WIDE, extra=()):
    values, specs, scratch, plan, sems = [], [], [], [], 0

    def far(shape, dtype, cuts, by_rows, start=0):
        nonlocal sems
        scratch.append(pltpu.VMEM(shape, dtype))
        sems += len(cuts or (0,))
        return len(scratch) - 1, sems - len(cuts or (0,)), cuts, by_rows, start

    for operand in operands:
        if isinstance(operand, In):
            values.append(operand.value)
            specs.append(THERE)
            plan.append(far(operand.shape, operand.value.dtype, operand.cuts, operand.by_rows, operand.start))
        elif isinstance(operand, After):
            values.append(operand.value)
            specs.append(THERE)
            plan.append(None)
        else:
            value, spec = operand if isinstance(operand, tuple) else (operand, HERE)
            values.append(value)
            specs.append(spec)
            plan.append(())
    shapes, out_specs = [], []
    for out in outs:
        if isinstance(out, Out):
            shapes.append(jax.ShapeDtypeStruct((out.rows, out.shape[1]), out.dtype))
            out_specs.append(THERE)
            plan.append(far(out.shape, out.dtype, out.cuts, out.by_rows))
        else:
            shapes.append(jax.ShapeDtypeStruct(*out))
            out_specs.append(HERE)
            plan.append(())

    def run(*refs):
        inner, waiting = [], []
        mine = refs[len(values) + len(outs) :]
        for at, (ref, how) in enumerate(zip(refs, plan)):
            if how is None:
                continue
            if how == ():
                inner.append(ref)
                continue
            inner.append(Far(ref, mine[how[0]], mine[-1], *how[1:]))
            if at >= len(values):
                waiting.append(inner[-1])
        kernel(*inner, *mine[len(scratch) : len(scratch) + len(extra)])
        for one in waiting:
            one.wait()

    return pl.pallas_call(
        run,
        name=name,
        out_shape=shapes,
        in_specs=specs,
        out_specs=out_specs,
        scratch_shapes=scratch + list(extra) + ([pltpu.SemaphoreType.DMA((sems,))] if sems else []),
        compiler_params=pltpu.CompilerParams(vmem_limit_bytes=limit),
        cost_estimate=pl.CostEstimate(flops=cost * MICRO, bytes_accessed=1000, transcendentals=0),
    )(*values)


def flat(ref):
    value = ref[...].astype(F32)
    return value.reshape(value.shape[0] * value.shape[1], D).astype(BF)


def split(value, yl):
    low, high = value[:, :SLOTS, :], value[:, SLOTS:, :]
    rows = value.shape[0] * SLOTS
    ours = jnp.where(yl == 0, low, high).reshape(rows, D)
    theirs = jnp.where(yl == 0, high, low).reshape(rows, D)
    return ours, theirs


def merge(ours, theirs, yl):
    groups = (ours.shape[0] // SLOTS, SLOTS, D)
    ours, theirs = ours.reshape(groups), theirs.reshape(groups)
    low, high = jnp.where(yl == 0, ours, theirs), jnp.where(yl == 0, theirs, ours)
    return jnp.concatenate([low, high], axis=1)


def softmax(scores, axis):
    raised = jnp.exp(scores - jnp.max(scores, axis=axis, keepdims=True))
    return raised / jnp.sum(raised, axis=axis, keepdims=True)


def softmax_back(share, share_grad, axis):
    return share * (share_grad - jnp.sum(share_grad * share, axis=axis, keepdims=True))


def front(place, patches, own, other, rows, dispatch, keys):
    patches.fetch()
    core = place[0]
    for at, block in ((core, own), (1 - core, other)):
        keys.here[pl.ds(pl.multiple_of(at * 256, 256), 256), :] = flat(block)
    keys.copy(0, True).start()
    image = patches.get()
    share = softmax(dot_last(image, keys.here[...]), 0)
    dispatch.put(share)
    rows.put(dot_rows(share.astype(BF), image).astype(BF))


def front_grads(patches, keys, out_grad, grads, combine):
    patches.fetch()
    keys.fetch()
    out_grad.fetch()
    share = softmax(dot_last(patches.get(), keys.get()), 1)
    combine.put(share)
    grads.put(dot_rows(share.astype(BF), out_grad.get()).astype(BF))


def part_ways(place, routed, ours, theirs):
    near, far = split(routed[...].astype(F32), place[1])
    ours[...] = near.astype(BF)
    theirs[...] = far.astype(BF)


def begin(*fars):
    for piece in range(2):
        for far in fars:
            far.fetch(piece)


def arrived(step, *fars):
    if step < 2:
        for far in fars:
            far.copy(step, False).wait()


def add(total, term):
    return term if total is None else total + term


def forward(*refs):
    blocks = (len(refs) - 3) // 2
    low, first, second, outs, acts = refs[:blocks], *refs[blocks : blocks + 2], refs[-blocks - 1 : -1], refs[-1]
    begin(first, second)
    here = jnp.concatenate([ref[...] for ref in low], axis=0)
    acts.put(here, 0)
    total = None
    for step in range(first.here.shape[1] // TILE):
        arrived(step, first)
        part = slice(step * TILE, step * TILE + TILE)
        value = dot(here, first.here[:, part])
        square = value * value
        bend = jnp.tanh(ROOT * value * (1.0 + CUBIC * square))
        gate = 0.5 + 0.5 * bend
        active = (value * gate).astype(BF)
        acts.put(active, 1 + step)
        rise = (0.5 * ROOT) * value * (1.0 - bend * bend) * (1.0 + (3.0 * CUBIC) * square)
        acts.put((gate + rise).astype(BF), 1 + first.here.shape[1] // TILE + step)
        arrived(step, second)
        if step > 0:
            total = add(total, dot(before, second.here[past, :]))
        before, past = active, part
    total = add(total, dot(before, second.here[past, :]))
    for at, out in enumerate(outs):
        out[...] = total[at * 256 : at * 256 + 256].astype(out.dtype)


def backward(*refs):
    blocks = (len(refs) - 4) // 2
    low, first, second, slope, outs, kept = (
        refs[:blocks], *refs[blocks : blocks + 3], refs[-blocks - 1 : -1], refs[-1],
    )
    begin(second, slope, first)
    here = jnp.concatenate([ref[...] for ref in low], axis=0)
    kept.put(here, 0)
    total = None
    for step in range(first.here.shape[1] // TILE):
        arrived(step, second, slope)
        part = slice(step * TILE, step * TILE + TILE)
        rounded = (dot_last(here, second.here[part, :]) * slope.here[:, part].astype(F32)).astype(BF)
        kept.put(rounded, 1 + step)
        arrived(step, first)
        if step > 0:
            total = add(total, dot_last(before, first.here[:, past]))
        before, past = rounded, part
    total = add(total, dot_last(before, first.here[:, past]))
    for at, out in enumerate(outs):
        out[...] = total[at * 256 : at * 256 + 256].astype(out.dtype)


def weight_grad(steps, into, *refs):
    acts, kept, out, done = refs[:3], refs[3:6], refs[6], refs[7]
    done[...] = jnp.zeros((8, 128), F32)
    narrow = [1 + step for step in range(steps)] if not into else [0]
    other = [0] if not into else [1 + step for step in range(steps)]
    for step in range(steps):
        for act, keep in zip(acts, kept):
            if step == 0 or not into:
                act.fetch(narrow[0 if into else step])
            if step == 0 or into:
                keep.fetch(other[step if into else 0])
    held = [(keep if not into else act).get(0) for act, keep in zip(acts, kept)]
    for step in range(steps):
        part = slice(step * TILE, step * TILE + TILE)
        total = None
        for act, keep, one in zip(acts, kept, held):
            moving = keep.get(other[step]) if into else act.get(narrow[step])
            term = dot_rows(one, moving) if into else dot_rows(moving, one)
            total = term if total is None else total + term
        if into:
            out[:, part] = total.astype(BF)
        else:
            out[part, :] = total.astype(BF)


def join(place, ours, ours_far, theirs, theirs_far, out):
    near = ours[...] + ours_far[...].astype(F32)
    far = theirs[...].astype(F32) + theirs_far[...].astype(F32)
    out[...] = merge(near, far, place[1]).astype(BF)


def middle(slot_output, out_grad, combine, layer_out, mix):
    out_grad.fetch()
    combine.fetch()
    grad = dot_last(out_grad.get(), slot_output[...])
    share = combine.get()
    mix.put(softmax_back(share, grad, 1))
    layer_out.put(dot(share.astype(BF), slot_output[...]).astype(BF))


def last(place, slot_in_grad, patches, dispatch, mix, score_grad, kept, sent, term):
    patches.fetch()
    dispatch.fetch()
    mix.fetch()
    image = patches.get()
    grad = dot_last(image, slot_in_grad[...])
    change = softmax_back(dispatch.get(), grad, 0)
    score = (mix.get() + change).astype(BF)
    score_grad.put(score)
    term[...] = dot_rows(score, image)
    core = place[0]
    kept[...] = term[pl.ds(pl.multiple_of(core * 256, 256), 256), :]
    sent[...] = term[pl.ds(pl.multiple_of((1 - core) * 256, 256), 256), :].astype(BF)


def fold(mine, other, out):
    out[...] = (mine[...] + other[...].astype(F32)).reshape(64, SLOTS, D).astype(BF)


def patch_back(dispatch, slots, score_grad, keys, out):
    dispatch.fetch()
    score_grad.fetch()
    keys.fetch()
    total = dot(dispatch.get().astype(BF), slots[...])
    out.put((total + dot(score_grad.get(), keys.get())).astype(BF))


def swap(value, axis):
    return lax.ppermute(value, axis, [(0, 1), (1, 0)])


def hop(value, flips):
    return lax.ppermute(value, ("dp", "yl"), [(at, at ^ flips) for at in range(4)])


NEXT, ACROSS, AROUND = 1, 2, 3


def exchange(value, axes):
    return lax.all_to_all(value, axes, split_axis=0, concat_axis=0, tiled=True)


def route(rows):
    return exchange(rows.reshape(64, 2 * SLOTS, D), ROUTE)


def local(patches, slot_keys, expert_in, expert_out, out_grad):
    first, second = expert_in[0], expert_out[0]
    half = first.shape[1]
    steps = half // TILE
    place = jnp.stack([lax.axis_index("core"), lax.axis_index("yl")]).astype(jnp.int32)
    place = (place, FLAG)
    block, full, final = ((256, D), BF), ((512, D), BF), ((256, D), F32)
    share = Out((256, 512), F32, room=True)

    own = exchange(jnp.broadcast_to(slot_keys[None], (64, SLOTS, D)), PLANE)
    rows, dispatch, keys = call(
        front, "front", 3, [Out(*full), share, Out(*full, room=True)],
        place, In(patches), own, swap(own, "core"), limit=TIGHT,
    )
    rows = route(rows)
    grads, combine = call(
        front_grads, "front_grads", 2, [Out(*full), share], In(patches), In(keys, 512), In(out_grad)
    )
    early, grads = grads, route(grads)

    def inward(routed, *after):
        return call(part_ways, "part_ways", 1, [block, block], place, routed, *after)

    act_cuts, kept_cuts = [(0, D)], [(0, D)]
    for step in range(2 * steps):
        act_cuts += [(D + TILE * step, D + TILE * (step + 1))]
    kept_cuts += act_cuts[1 : 1 + steps]
    slope_at = D + half
    pieces = [(0, TILE), (TILE, half)]
    fetched = In(first, cuts=pieces), In(second, cuts=pieces, by_rows=True)

    def ahead(name, blocks, outs, *after):
        rows = 256 * len(blocks)
        acts = Out((rows, D + 2 * half), BF, act_cuts, room=True)
        return call(forward, name, 60 if name == "forward_near" else 0, outs + [acts], *blocks, *fetched, *after, limit=TIGHT)

    def back(name, blocks, outs, acts, *after):
        rows = 256 * len(blocks)
        kept = Out((rows, D + half), BF, kept_cuts, room=True)
        slope = In(acts, rows, pieces, start=slope_at, width=half)
        cost = 60 if name == "backward_across" else 0
        return call(backward, name, cost, outs + [kept], *blocks, *fetched, slope, *after, limit=TIGHT)

    def outward(across, near, around):
        return hop(across, ACROSS), hop(near, NEXT), hop(around, AROUND)

    def join_up(name, *operands):
        return call(join, name, 20, [((64, 2 * SLOTS, D), BF)], place, *operands)[0]

    ours, theirs = inward(rows, After(early))
    near, around = hop(theirs, NEXT), hop(theirs, AROUND)
    across_out, acts_across = ahead("forward_across", [hop(ours, ACROSS)], [block])
    near_out, around_out, acts_near = ahead(
        "forward_near", [near, around], [block, block], After(acts_across)
    )
    ours_out, acts_ours = ahead("forward_ours", [ours], [final], After(acts_near))

    ours, theirs = inward(grads, After(acts_ours))
    received = outward(across_out, near_out, around_out)
    ours, theirs, *received = lax.optimization_barrier((ours, theirs, *received))
    near, around, across = hop(theirs, NEXT), hop(theirs, AROUND), hop(ours, ACROSS)
    out = join_up("join_out", ours_out, *received)
    slot_output = route(out).reshape(512, D)
    near_in, around_in, kept_near = back(
        "backward_near", [near, around], [block, block], acts_near, After(out)
    )
    across_in, kept_across = back(
        "backward_across", [across], [block], acts_across, After(kept_near)
    )
    ours_in, kept_ours = back("backward_ours", [ours], [final], acts_ours, After(kept_across))
    into = join_up("join_in", ours_in, *outward(across_in, near_in, around_in), After(slot_output))
    slot_in_grad = route(into).reshape(512, D)

    def weight_sum(name, towards, shape):
        pairs = ((acts_ours, kept_ours, 256), (acts_near, kept_near, 512), (acts_across, kept_across, 256))
        return call(
            lambda *refs: weight_grad(steps, towards, *refs), name, 4, [(shape, BF), ((8, 128), F32)],
            *[In(acts, rows, act_cuts) for acts, _, rows in pairs],
            *[In(kept, rows, kept_cuts) for _, kept, rows in pairs],
        )

    second_grad, second_done = weight_sum("second_grad", False, (half, D))
    first_grad, first_done = weight_sum("first_grad", True, (D, half))

    layer_out, mix = call(
        middle, "middle", 2, [Out(*block), share], slot_output, In(out_grad), In(combine, 256)
    )
    score_grad, kept, sent = call(
        last, "last", 3, [Out((256, 512), BF, room=True), final, block],
        place, slot_in_grad, In(patches), In(dispatch, 256), In(mix, 256),
        After(first_done), After(second_done), extra=(pltpu.VMEM((512, D), F32),),
    )
    (folded,) = call(fold, "fold", 1, [((64, SLOTS, D), BF)], kept, swap(sent, "core"))
    own_total = jnp.sum(exchange(folded, PLANE).astype(F32), axis=0)
    (patch_grad,) = call(
        patch_back, "patch_back", 2, [Out(*block)],
        In(dispatch, 256), slot_in_grad, In(score_grad, 256), In(keys, 512),
    )
    own_total, patch_grad = lax.optimization_barrier((own_total, patch_grad))
    slot_key_grad = own_total + swap(own_total, "dp")
    return layer_out, patch_grad, slot_key_grad, first_grad[None], second_grad[None]


def solution(mesh):
    fine = Mesh(mesh.devices.reshape(2, 2, 8, 4, 2), TOKEN)
    return jax.shard_map(
        local,
        mesh=fine,
        in_specs=(
            P(TOKEN, None),
            P(EXPERT, None),
            P(EXPERT, None, "dp"),
            P(EXPERT, "dp", None),
            P(TOKEN, None),
        ),
        out_specs=(
            P(TOKEN, None),
            P(TOKEN, None),
            P(EXPERT, None),
            P(EXPERT, None, "dp"),
            P(EXPERT, "dp", None),
        ),
        check_vma=False,
    )
```

```python
import jax
import jax.numpy as jnp
from jax import lax
from jax.experimental import pallas as pl
from jax.experimental.pallas import tpu as pltpu
from jax.sharding import Mesh, PartitionSpec as P

D = 768
SLOTS = 4
BF = jnp.bfloat16
F32 = jnp.float32
EXPERT = ("yl", "z", "x", "core")
TOKEN = ("dp",) + EXPERT
ROUTE = ("core", "z", "x")
PLANE = ("z", "x", "yl")
TILE = 256
WIDE, TIGHT = 46 * 1024 * 1024, 52 * 1024 * 1024
SPARE = 8000000
MICRO = 1000000000
CUBIC = 0.044715
ROOT = 0.7978845608028654


def mm(left, right, contract):
    return lax.dot_general(left, right, (contract, ((), ())), preferred_element_type=F32)


def dot(left, right):
    return mm(left, right, ((1,), (0,)))


def dot_rows(left, right):
    return mm(left, right, ((0,), (0,)))


def dot_last(left, right):
    return mm(left, right, ((1,), (1,)))


class Far:
    def __init__(self, there, here, sems, first_sem, cuts, by_rows, start):
        self.there, self.here, self.sems, self.first_sem = there, here, sems, first_sem
        self.cuts, self.by_rows, self.start = cuts, by_rows, start

    def copy(self, piece, out):
        rows, cols = self.here.shape
        start, stop = self.cuts[piece] if self.cuts else (0, cols)
        at = (pl.ds(0, rows), pl.ds(start, stop - start))
        if self.by_rows:
            at = (pl.ds(start, stop - start), pl.ds(0, cols))
        near = self.here.at[at]
        far = self.there.at[at[0], pl.ds(self.start + start, stop - start)] if self.start else self.there.at[at]
        source, target = (near, far) if out else (far, near)
        return pltpu.make_async_copy(source, target, self.sems.at[self.first_sem + piece])

    def fetch(self, *pieces):
        for piece in pieces or (0,):
            self.copy(piece, False).start()

    def get(self, piece=0):
        self.copy(piece, False).wait()
        start, stop = self.cuts[piece] if self.cuts else (0, self.here.shape[1])
        return self.here[:, start:stop]

    def put(self, value, piece=0):
        start, stop = self.cuts[piece] if self.cuts else (0, self.here.shape[1])
        self.here[:, start:stop] = value
        self.copy(piece, True).start()

    def wait(self):
        for piece in range(len(self.cuts or (0,))):
            self.copy(piece, True).wait()


HERE = pl.BlockSpec(memory_space=pltpu.VMEM)
FLAG = pl.BlockSpec(memory_space=pltpu.SMEM)
THERE = pl.BlockSpec(memory_space=pl.ANY)


class In:
    def __init__(self, value, rows=None, cuts=None, by_rows=False, start=0, width=None):
        self.value, self.cuts, self.by_rows, self.start = value, cuts, by_rows, start
        self.shape = (rows or value.shape[0], width or value.shape[1])


class After:
    def __init__(self, value):
        self.value = value


class Out:
    def __init__(self, shape, dtype, cuts=None, room=False, by_rows=False):
        self.shape, self.dtype, self.cuts, self.by_rows = shape, dtype, cuts, by_rows
        width = shape[1] * jnp.dtype(dtype).itemsize
        self.rows = max(shape[0], -(-SPARE // width) // 256 * 256 + 256) if room else shape[0]


def call(kernel, name, cost, outs, *operands, limit=WIDE, extra=()):
    values, specs, scratch, plan, sems = [], [], [], [], 0

    def far(shape, dtype, cuts, by_rows, start=0):
        nonlocal sems
        scratch.append(pltpu.VMEM(shape, dtype))
        sems += len(cuts or (0,))
        return len(scratch) - 1, sems - len(cuts or (0,)), cuts, by_rows, start

    for operand in operands:
        if isinstance(operand, In):
            values.append(operand.value)
            specs.append(THERE)
            plan.append(far(operand.shape, operand.value.dtype, operand.cuts, operand.by_rows, operand.start))
        elif isinstance(operand, After):
            values.append(operand.value)
            specs.append(THERE)
            plan.append(None)
        else:
            value, spec = operand if isinstance(operand, tuple) else (operand, HERE)
            values.append(value)
            specs.append(spec)
            plan.append(())
    shapes, out_specs = [], []
    for out in outs:
        if isinstance(out, Out):
            shapes.append(jax.ShapeDtypeStruct((out.rows, out.shape[1]), out.dtype))
            out_specs.append(THERE)
            plan.append(far(out.shape, out.dtype, out.cuts, out.by_rows))
        else:
            shapes.append(jax.ShapeDtypeStruct(*out))
            out_specs.append(HERE)
            plan.append(())

    def run(*refs):
        inner, waiting = [], []
        mine = refs[len(values) + len(outs) :]
        for at, (ref, how) in enumerate(zip(refs, plan)):
            if how is None:
                continue
            if how == ():
                inner.append(ref)
                continue
            inner.append(Far(ref, mine[how[0]], mine[-1], *how[1:]))
            if at >= len(values):
                waiting.append(inner[-1])
        kernel(*inner, *mine[len(scratch) : len(scratch) + len(extra)])
        for one in waiting:
            one.wait()

    return pl.pallas_call(
        run,
        name=name,
        out_shape=shapes,
        in_specs=specs,
        out_specs=out_specs,
        scratch_shapes=scratch + list(extra) + ([pltpu.SemaphoreType.DMA((sems,))] if sems else []),
        compiler_params=pltpu.CompilerParams(vmem_limit_bytes=limit),
        cost_estimate=pl.CostEstimate(flops=cost * MICRO, bytes_accessed=1000, transcendentals=0),
    )(*values)


def flat(ref):
    value = ref[...].astype(F32)
    return value.reshape(value.shape[0] * value.shape[1], D).astype(BF)


def split(value, yl):
    low, high = value[:, :SLOTS, :], value[:, SLOTS:, :]
    rows = value.shape[0] * SLOTS
    ours = jnp.where(yl == 0, low, high).reshape(rows, D)
    theirs = jnp.where(yl == 0, high, low).reshape(rows, D)
    return ours, theirs


def merge(ours, theirs, yl):
    groups = (ours.shape[0] // SLOTS, SLOTS, D)
    ours, theirs = ours.reshape(groups), theirs.reshape(groups)
    low, high = jnp.where(yl == 0, ours, theirs), jnp.where(yl == 0, theirs, ours)
    return jnp.concatenate([low, high], axis=1)


def softmax(scores, axis):
    raised = jnp.exp(scores - jnp.max(scores, axis=axis, keepdims=True))
    return raised / jnp.sum(raised, axis=axis, keepdims=True)


def softmax_back(share, share_grad, axis):
    return share * (share_grad - jnp.sum(share_grad * share, axis=axis, keepdims=True))


def front(place, patches, own, other, rows, dispatch, keys):
    patches.fetch()
    core = place[0]
    for at, block in ((core, own), (1 - core, other)):
        keys.here[pl.ds(pl.multiple_of(at * 256, 256), 256), :] = flat(block)
    keys.copy(0, True).start()
    image = patches.get()
    share = softmax(dot_last(image, keys.here[...]), 0)
    dispatch.put(share)
    rows.put(dot_rows(share.astype(BF), image).astype(BF))


def front_grads(patches, keys, out_grad, grads, combine):
    patches.fetch()
    keys.fetch()
    out_grad.fetch()
    share = softmax(dot_last(patches.get(), keys.get()), 1)
    combine.put(share)
    grads.put(dot_rows(share.astype(BF), out_grad.get()).astype(BF))


def part_ways(place, routed, ours, theirs):
    near, far = split(routed[...].astype(F32), place[1])
    ours[...] = near.astype(BF)
    theirs[...] = far.astype(BF)


def begin(*fars):
    for piece in range(2):
        for far in fars:
            far.fetch(piece)


def arrived(step, *fars):
    if step < 2:
        for far in fars:
            far.copy(step, False).wait()


def add(total, term):
    return term if total is None else total + term


def forward(*refs):
    blocks = (len(refs) - 3) // 2
    low, first, second, outs, acts = refs[:blocks], *refs[blocks : blocks + 2], refs[-blocks - 1 : -1], refs[-1]
    begin(first, second)
    here = jnp.concatenate([ref[...] for ref in low], axis=0)
    acts.put(here, 0)
    total = None
    for step in range(first.here.shape[1] // TILE):
        arrived(step, first)
        part = slice(step * TILE, step * TILE + TILE)
        value = dot(here, first.here[:, part])
        square = value * value
        bend = jnp.tanh(ROOT * value * (1.0 + CUBIC * square))
        gate = 0.5 + 0.5 * bend
        active = (value * gate).astype(BF)
        acts.put(active, 1 + step)
        rise = (0.5 * ROOT) * value * (1.0 - bend * bend) * (1.0 + (3.0 * CUBIC) * square)
        acts.put((gate + rise).astype(BF), 1 + first.here.shape[1] // TILE + step)
        arrived(step, second)
        if step > 0:
            total = add(total, dot(before, second.here[past, :]))
        before, past = active, part
    total = add(total, dot(before, second.here[past, :]))
    for at, out in enumerate(outs):
        out[...] = total[at * 256 : at * 256 + 256].astype(out.dtype)


def backward(*refs):
    blocks = (len(refs) - 4) // 2
    low, first, second, slope, outs, kept = (
        refs[:blocks], *refs[blocks : blocks + 3], refs[-blocks - 1 : -1], refs[-1],
    )
    begin(second, slope, first)
    here = jnp.concatenate([ref[...] for ref in low], axis=0)
    kept.put(here, 0)
    total = None
    for step in range(first.here.shape[1] // TILE):
        arrived(step, second, slope)
        part = slice(step * TILE, step * TILE + TILE)
        rounded = (dot_last(here, second.here[part, :]) * slope.here[:, part].astype(F32)).astype(BF)
        kept.put(rounded, 1 + step)
        arrived(step, first)
        if step > 0:
            total = add(total, dot_last(before, first.here[:, past]))
        before, past = rounded, part
    total = add(total, dot_last(before, first.here[:, past]))
    for at, out in enumerate(outs):
        out[...] = total[at * 256 : at * 256 + 256].astype(out.dtype)


def weight_grad(steps, into, *refs):
    acts, kept, out, done = refs[:3], refs[3:6], refs[6], refs[7]
    done[...] = jnp.zeros((8, 128), F32)
    narrow = [1 + step for step in range(steps)] if not into else [0]
    other = [0] if not into else [1 + step for step in range(steps)]
    for step in range(steps):
        for act, keep in zip(acts, kept):
            if step == 0 or not into:
                act.fetch(narrow[0 if into else step])
            if step == 0 or into:
                keep.fetch(other[step if into else 0])
    held = [(keep if not into else act).get(0) for act, keep in zip(acts, kept)]
    for step in range(steps):
        part = slice(step * TILE, step * TILE + TILE)
        total = None
        for act, keep, one in zip(acts, kept, held):
            moving = keep.get(other[step]) if into else act.get(narrow[step])
            term = dot_rows(one, moving) if into else dot_rows(moving, one)
            total = term if total is None else total + term
        if into:
            out[:, part] = total.astype(BF)
        else:
            out[part, :] = total.astype(BF)


def join(place, ours, ours_far, theirs, theirs_far, out):
    near = ours[...] + ours_far[...].astype(F32)
    far = theirs[...].astype(F32) + theirs_far[...].astype(F32)
    out[...] = merge(near, far, place[1]).astype(BF)


def middle(slot_output, out_grad, combine, layer_out, mix):
    out_grad.fetch()
    combine.fetch()
    grad = dot_last(out_grad.get(), slot_output[...])
    share = combine.get()
    mix.put(softmax_back(share, grad, 1))
    layer_out.put(dot(share.astype(BF), slot_output[...]).astype(BF))


def last(place, slot_in_grad, patches, dispatch, mix, score_grad, kept, sent, term):
    patches.fetch()
    dispatch.fetch()
    mix.fetch()
    image = patches.get()
    grad = dot_last(image, slot_in_grad[...])
    change = softmax_back(dispatch.get(), grad, 0)
    score = (mix.get() + change).astype(BF)
    score_grad.put(score)
    term[...] = dot_rows(score, image)
    core = place[0]
    kept[...] = term[pl.ds(pl.multiple_of(core * 256, 256), 256), :]
    sent[...] = term[pl.ds(pl.multiple_of((1 - core) * 256, 256), 256), :].astype(BF)


def fold(mine, other, out):
    out[...] = (mine[...] + other[...].astype(F32)).reshape(64, SLOTS, D).astype(BF)


def patch_back(dispatch, slots, score_grad, keys, out):
    dispatch.fetch()
    score_grad.fetch()
    keys.fetch()
    total = dot(dispatch.get().astype(BF), slots[...])
    out.put((total + dot(score_grad.get(), keys.get())).astype(BF))


def swap(value, axis):
    return lax.ppermute(value, axis, [(0, 1), (1, 0)])


def hop(value, flips):
    return lax.ppermute(value, ("dp", "yl"), [(at, at ^ flips) for at in range(4)])


NEXT, ACROSS, AROUND = 1, 2, 3


def exchange(value, axes):
    return lax.all_to_all(value, axes, split_axis=0, concat_axis=0, tiled=True)


def route(rows):
    return exchange(rows.reshape(64, 2 * SLOTS, D), ROUTE)


def local(patches, slot_keys, expert_in, expert_out, out_grad):
    first, second = expert_in[0], expert_out[0]
    half = first.shape[1]
    steps = half // TILE
    place = jnp.stack([lax.axis_index("core"), lax.axis_index("yl")]).astype(jnp.int32)
    place = (place, FLAG)
    block, full, final = ((256, D), BF), ((512, D), BF), ((256, D), F32)
    share = Out((256, 512), F32, room=True)

    own = exchange(jnp.broadcast_to(slot_keys[None], (64, SLOTS, D)), PLANE)
    rows, dispatch, keys = call(
        front, "front", 3, [Out(*full), share, Out(*full, room=True)],
        place, In(patches), own, swap(own, "core"), limit=TIGHT,
    )
    rows = route(rows)
    grads, combine = call(
        front_grads, "front_grads", 2, [Out(*full), share], In(patches), In(keys, 512), In(out_grad)
    )
    early, grads = grads, route(grads)

    def inward(routed, *after):
        return call(part_ways, "part_ways", 1, [block, block], place, routed, *after)

    act_cuts, kept_cuts = [(0, D)], [(0, D)]
    for step in range(2 * steps):
        act_cuts += [(D + TILE * step, D + TILE * (step + 1))]
    kept_cuts += act_cuts[1 : 1 + steps]
    slope_at = D + half
    pieces = [(0, TILE), (TILE, half)]
    fetched = In(first, cuts=pieces), In(second, cuts=pieces, by_rows=True)

    def ahead(name, blocks, outs, *after):
        rows = 256 * len(blocks)
        acts = Out((rows, D + 2 * half), BF, act_cuts, room=True)
        return call(forward, name, 60 if name == "forward_near" else 0, outs + [acts], *blocks, *fetched, *after, limit=TIGHT)

    def back(name, blocks, outs, acts, *after):
        rows = 256 * len(blocks)
        kept = Out((rows, D + half), BF, kept_cuts, room=True)
        slope = In(acts, rows, pieces, start=slope_at, width=half)
        cost = 60 if name == "backward_across" else 0
        return call(backward, name, cost, outs + [kept], *blocks, *fetched, slope, *after, limit=TIGHT)

    def outward(across, near, around):
        return hop(across, ACROSS), hop(near, NEXT), hop(around, AROUND)

    def join_up(name, *operands):
        return call(join, name, 20, [((64, 2 * SLOTS, D), BF)], place, *operands)[0]

    ours, theirs = inward(rows, After(early))
    near, around = hop(theirs, NEXT), hop(theirs, AROUND)
    across_out, acts_across = ahead("forward_across", [hop(ours, ACROSS)], [block])
    near_out, around_out, acts_near = ahead(
        "forward_near", [near, around], [block, block], After(acts_across)
    )
    ours_out, acts_ours = ahead("forward_ours", [ours], [final], After(acts_near))

    ours, theirs = inward(grads, After(acts_ours))
    received = outward(across_out, near_out, around_out)
    *early, last_in = received
    ours, theirs, *early = lax.optimization_barrier((ours, theirs, *early))
    near, around, across = hop(theirs, NEXT), hop(theirs, AROUND), hop(ours, ACROSS)
    out = join_up("join_out", ours_out, *early, last_in)
    slot_output = route(out).reshape(512, D)
    near_in, around_in, kept_near = back(
        "backward_near", [near, around], [block, block], acts_near, After(out)
    )
    across_in, kept_across = back(
        "backward_across", [across], [block], acts_across, After(kept_near)
    )
    ours_in, kept_ours = back("backward_ours", [ours], [final], acts_ours, After(kept_across))
    into = join_up("join_in", ours_in, *outward(across_in, near_in, around_in), After(slot_output))
    slot_in_grad = route(into).reshape(512, D)

    def weight_sum(name, towards, shape):
        pairs = ((acts_ours, kept_ours, 256), (acts_near, kept_near, 512), (acts_across, kept_across, 256))
        return call(
            lambda *refs: weight_grad(steps, towards, *refs), name, 4, [(shape, BF), ((8, 128), F32)],
            *[In(acts, rows, act_cuts) for acts, _, rows in pairs],
            *[In(kept, rows, kept_cuts) for _, kept, rows in pairs],
        )

    second_grad, second_done = weight_sum("second_grad", False, (half, D))
    first_grad, first_done = weight_sum("first_grad", True, (D, half))

    layer_out, mix = call(
        middle, "middle", 2, [Out(*block), share], slot_output, In(out_grad), In(combine, 256)
    )
    score_grad, kept, sent = call(
        last, "last", 3, [Out((256, 512), BF, room=True), final, block],
        place, slot_in_grad, In(patches), In(dispatch, 256), In(mix, 256),
        After(first_done), After(second_done), extra=(pltpu.VMEM((512, D), F32),),
    )
    (folded,) = call(fold, "fold", 1, [((64, SLOTS, D), BF)], kept, swap(sent, "core"))
    own_total = jnp.sum(exchange(folded, PLANE).astype(F32), axis=0)
    (patch_grad,) = call(
        patch_back, "patch_back", 2, [Out(*block)],
        In(dispatch, 256), slot_in_grad, In(score_grad, 256), In(keys, 512),
    )
    own_total, patch_grad = lax.optimization_barrier((own_total, patch_grad))
    slot_key_grad = own_total + swap(own_total, "dp")
    return layer_out, patch_grad, slot_key_grad, first_grad[None], second_grad[None]


def solution(mesh):
    fine = Mesh(mesh.devices.reshape(2, 2, 8, 4, 2), TOKEN)
    return jax.shard_map(
        local,
        mesh=fine,
        in_specs=(
            P(TOKEN, None),
            P(EXPERT, None),
            P(EXPERT, None, "dp"),
            P(EXPERT, "dp", None),
            P(TOKEN, None),
        ),
        out_specs=(
            P(TOKEN, None),
            P(TOKEN, None),
            P(EXPERT, None),
            P(EXPERT, None, "dp"),
            P(EXPERT, "dp", None),
        ),
        check_vma=False,
    )
```
